512 devices in a mesh: ctx: 128 (over z, y, core), head: 4 (over x).
Axes of the slice: x: 4, y: 8, z: 8, core: 2. Of those that a mesh axis runs over, the one named last changes fastest.
Arguments:
- tokens: bfloat16 [32768, 1024], P('ctx', 'head'), may hold values from -6 to 6
- q_weight: bfloat16 [1024, 1024], P(None, 'head'), may hold values from -0.1875 to 0.1875
- k_weight: bfloat16 [1024, 1024], P(None, 'head'), may hold values from -0.1875 to 0.1875
- v_weight: bfloat16 [1024, 2048], P(None, 'head'), may hold values from -0.1875 to 0.1875
- z_weight: bfloat16 [1024, 2048], P(None, 'head'), may hold values from -0.1875 to 0.1875
- a_weight: bfloat16 [1024, 16], P(None, 'head'), may hold values from -0.1875 to 0.1875
- b_weight: bfloat16 [1024, 16], P(None, 'head'), may hold values from -0.1875 to 0.1875
- conv_q: float32 [4, 1024], P(None, 'head'), may hold values from -3 to 3
- conv_k: float32 [4, 1024], P(None, 'head'), may hold values from -3 to 3
- conv_v: float32 [4, 2048], P(None, 'head'), may hold values from -3 to 3
- decay_rate: float32 [16], P('head'), may hold values from 0.5 to 16
- dt_bias: float32 [16], P('head'), may hold values from -9 to -3
- norm_gain: float32 [128], replicated, may hold values from 0.1 to 1.9
- out_weight: bfloat16 [2048, 1024], P('head'), may hold values from -0.125 to 0.125
- doc_lengths: int32 [64], replicated, may hold values from 1 to 1024, 32768 in all
Outputs:
- mixed: bfloat16 [32768, 1024], P('ctx', 'head')
The draws below stay inside these ranges and needn't reach their ends.
Inputs may be any that keep to these rules, and one draw needn't show every extreme that they name: `doc_lengths`: 64 document lengths summing to 32768; the longest is exactly 1024.
All inputs are finite; a program needn't handle non-finite values.
Results may differ from the reference program's by a relative error of at most 0.015.
Values may be sent and summed in bfloat16 or wider, within the bound.
A program may use at most 192 MiB of HBM per device.

```python
import math
import jax
import jax.numpy as jnp
import numpy as np
from jax import lax

D = 1024
HV = 16
HK = 8
DK = 128
DV = 128
CONV = 4
CH = 64
TOK_DEV = 256
TOKENS = 32768
DOCS = 64


def level_of(own_key, shape, pieces, least, largest):
    gain, own = 1.0, jax.random.fold_in(own_key, 6)
    for axis_at, shards_of in pieces:
        heights = jnp.exp(jax.random.uniform(jax.random.fold_in(own, axis_at), (shards_of,), jnp.float32, least / len(pieces), largest / len(pieces)))
        gain = gain * jnp.repeat(heights, shape[axis_at] // shards_of).reshape([-1 if axis == axis_at else 1 for axis in range(len(shape))])
    return gain


def split_up(number_of, total, limit, skew):
    portions = [(1 << 20) // math.isqrt(grade ** skew) + 1 for grade in range(2, number_of + 1)]
    surplus, counts = total - limit - (number_of - 1), [1] * (number_of - 1)
    while surplus > 0:
        free = [i for i in range(number_of - 1) if counts[i] < limit]
        pool, budget = sum([portions[i] for i in free]), surplus
        for i in free:
            extra = min(limit - counts[i], max(1, budget * portions[i] // pool), surplus)
            counts[i] = counts[i] + extra
            surplus = surplus - extra
    return np.array([limit] + counts)


def ragged(stream_key, number_of, total, bound, skew):
    if number_of == 2:
        one = jax.random.randint(stream_key, (), max(1, total - bound), min(bound, total - 1) + 1)
        return jnp.stack([one, total - one])
    sizes = jnp.asarray(split_up(number_of, total, bound, skew), jnp.int32)
    couples = (number_of - 1) // 2
    giver, taker = sizes[1:1 + 2 * couples:2], sizes[2:2 + 2 * couples:2]
    slack = jnp.minimum(giver - 1, bound - taker)
    shifted = jax.random.randint(jax.random.fold_in(stream_key, 1), (couples,), 0, 1 << 20) % (slack + 1)
    sizes = sizes.at[1:1 + 2 * couples:2].set(giver - shifted).at[2:2 + 2 * couples:2].set(taker + shifted)
    return sizes[jax.random.permutation(jax.random.fold_in(stream_key, 2), number_of)]


def bell_draw(key, extent, spread, bound, cuts=(), kind=jnp.bfloat16):
    loudness = level_of(key, extent, cuts, -0.22, 0.18) if cuts else 1.0
    array = jax.random.normal(key, extent, jnp.float32) * spread * loudness
    return jnp.minimum(jnp.maximum(array, -bound), bound).astype(kind)


def setup_inputs(seed: int = 0) -> dict:
    key_of = jax.random.split(jax.random.key(seed), 16)
    return {
        "tokens": bell_draw(key_of[0], (TOKENS, D), 1.0, 6.0, ((0, 128), (1, 4))),
        "q_weight": bell_draw(key_of[1], (D, HK * DK), D ** -0.5, 0.1875, ((1, 4),)),
        "k_weight": bell_draw(key_of[2], (D, HK * DK), D ** -0.5, 0.1875, ((1, 4),)),
        "v_weight": bell_draw(key_of[3], (D, HV * DV), D ** -0.5, 0.1875, ((1, 4),)),
        "z_weight": bell_draw(key_of[4], (D, HV * DV), D ** -0.5, 0.1875, ((1, 4),)),
        "a_weight": bell_draw(key_of[5], (D, HV), D ** -0.5, 0.1875, ((1, 4),)),
        "b_weight": bell_draw(key_of[6], (D, HV), D ** -0.5, 0.1875, ((1, 4),)),
        "conv_q": bell_draw(key_of[7], (CONV, HK * DK), CONV ** -0.5, 3.0, ((1, 4),), jnp.float32),
        "conv_k": bell_draw(key_of[8], (CONV, HK * DK), CONV ** -0.5, 3.0, ((1, 4),), jnp.float32),
        "conv_v": bell_draw(key_of[9], (CONV, HV * DV), CONV ** -0.5, 3.0, ((1, 4),), jnp.float32),
        "decay_rate": jnp.clip(jnp.exp(math.log(16.0) - 3.465736 * jax.random.uniform(key_of[10], (HV,), jnp.float32) ** level_of(key_of[10], (HV,), ((0, 4),), -0.2, 0.2)), 0.5, 16.0),
        "dt_bias": jnp.clip(-9.0 + 6.0 * jax.random.uniform(key_of[11], (HV,), jnp.float32) ** level_of(key_of[11], (HV,), ((0, 4),), -0.2, 0.2), -9.0, -3.0),
        "norm_gain": jnp.clip(1.0 + 0.18 * jax.random.normal(key_of[12], (DV,), jnp.float32), 0.1, 1.9),
        "out_weight": bell_draw(key_of[13], (HV * DV, D), (HV * DV) ** -0.5, 0.125, ((0, 4),)),
        "doc_lengths": ragged(key_of[14], DOCS, TOKENS, 4 * TOK_DEV, 2).astype(jnp.int32),
    }


highest = lax.Precision.HIGHEST

def segment_of(doc_lengths, positions):
    starts = (jnp.cumsum(doc_lengths) - doc_lengths).astype(jnp.int32)
    hits = (starts[None, :] <= positions[:, None]).astype(jnp.int32)
    return (lax.optimization_barrier(jnp.sum(hits, axis=1)) - 1).astype(jnp.int32)

def short_conv(inputs, before, segment, segment_before, kernel):
    kernel_len = kernel.shape[0]
    tok_rows = inputs.shape[0]
    padded = jnp.concatenate([before, inputs], axis=0).astype(jnp.float32)
    padded_seg = jnp.concatenate([segment_before, segment])
    summed = jnp.zeros(inputs.shape, jnp.float32)
    for tap_index in range(kernel_len):
        same_doc = (padded_seg[tap_index:tap_index + tok_rows] == segment)[:, None]
        summed = summed + jnp.where(same_doc, padded[tap_index:tap_index + tok_rows] * kernel[tap_index], 0.0)
    return jax.nn.silu(summed)

def unit_rows(matrix):
    return matrix / jnp.sqrt(lax.optimization_barrier(jnp.sum(matrix * matrix, axis=-1, keepdims=True)) + 1e-06)

def lower_inverse(system):
    block_len = system.shape[-1]
    axis_row = system.ndim - 2
    start_mat = jnp.broadcast_to(jnp.eye(block_len, dtype=jnp.float32), system.shape).astype(system.dtype)
    col_ids = lax.broadcasted_iota(jnp.int32, (block_len,), 0)

    def solve_row(row_index, inverse):
        coeffs = lax.dynamic_index_in_dim(system, row_index, axis=axis_row, keepdims=False)
        unit_row = (col_ids == row_index).astype(system.dtype)
        new_row = unit_row - jnp.einsum('...j,...jd->...d', coeffs, inverse, precision=highest)
        return lax.dynamic_update_index_in_dim(inverse, new_row, row_index, axis_row)
    return lax.fori_loop(1, block_len, solve_row, start_mat)

def block_terms(queries, keys, values, gate_log, write_rate, segment, segment_prior):
    block_len = gate_log.shape[-1]
    key_size = keys.shape[-1]
    cumulative = jnp.cumsum(gate_log, axis=-1)
    row_ids = lax.broadcasted_iota(jnp.int32, (block_len, block_len), 0)
    col_ids = lax.broadcasted_iota(jnp.int32, (block_len, block_len), 1)
    same_doc = segment[..., :, None] == segment[..., None, :]
    lower_mask = same_doc & (row_ids >= col_ids)
    strict = same_doc & (row_ids > col_ids)
    gap_log = cumulative[..., :, None] - cumulative[..., None, :]
    decays = jnp.exp(jnp.where(lower_mask, gap_log, -1e+30))
    strict_decay = jnp.where(strict, decays, 0.0)
    carried = jnp.where(segment == segment_prior[..., None], jnp.exp(cumulative), 0.0)
    key_dots = jnp.einsum('...id,...jd->...ij', keys, keys, precision=highest)
    system = write_rate[..., :, None] * strict_decay * key_dots
    inverse = lower_inverse(system)
    wy_keys = jnp.einsum('...ij,...jd->...id', inverse, (write_rate * carried)[..., None] * keys, precision=highest)
    wy_values = jnp.einsum('...ij,...jd->...id', inverse, write_rate[..., None] * values, precision=highest)
    scores = jnp.einsum('...id,...jd->...ij', queries, keys, precision=highest) * decays
    keys_last = keys * decays[..., block_len - 1, :][..., None]
    identity_mat = jnp.eye(key_size, dtype=jnp.float32)
    transition = carried[..., block_len - 1][..., None, None] * identity_mat - jnp.einsum('...jd,...je->...de', keys_last, wy_keys, precision=highest)
    offset = jnp.einsum('...jd,...je->...de', keys_last, wy_values, precision=highest)
    reader = queries * carried[..., None] - jnp.einsum('...ij,...jd->...id', scores, wy_keys, precision=highest)
    local_out = jnp.einsum('...ij,...jd->...id', scores, wy_values, precision=highest)
    return (reader, local_out, transition, offset)

def gated_norm(attended, z_in, norm_gain):
    gate_vals = z_in.astype(jnp.float32).reshape(attended.shape)
    root_mean = jnp.sqrt(lax.optimization_barrier(jnp.mean(attended * attended, axis=-1, keepdims=True)) + 1e-06)
    return attended / root_mean * norm_gain * jax.nn.silu(gate_vals)

def advance(carry_state, members):
    reader, local_out, transition, offset = members
    emitted = jnp.dot(reader, carry_state, precision=highest) + local_out
    return (jnp.dot(transition, carry_state, precision=highest) + offset, emitted)

def reference(tokens, q_weight, k_weight, v_weight, z_weight, a_weight, b_weight, conv_q, conv_k, conv_v, decay_rate, dt_bias, norm_gain, out_weight, doc_lengths):
    positions = jnp.arange(TOKENS, dtype=jnp.int32)
    segment = segment_of(doc_lengths, positions)

    def project(matrix):
        return jnp.dot(tokens, matrix, preferred_element_type=jnp.float32)
    q_in = project(q_weight).astype(jnp.bfloat16)
    k_in = project(k_weight).astype(jnp.bfloat16)
    v_in = project(v_weight).astype(jnp.bfloat16)
    z_in = project(z_weight).astype(jnp.bfloat16)
    a_proj = project(a_weight)
    b_proj = project(b_weight)
    segment_before = jnp.full((CONV - 1,), -1, jnp.int32)
    queries = short_conv(q_in, jnp.zeros((CONV - 1, HK * DK), jnp.bfloat16), segment, segment_before, conv_q)
    keys = short_conv(k_in, jnp.zeros((CONV - 1, HK * DK), jnp.bfloat16), segment, segment_before, conv_k)
    values = short_conv(v_in, jnp.zeros((CONV - 1, HV * DV), jnp.bfloat16), segment, segment_before, conv_v)
    group_size = HV // HK
    queries = jnp.repeat(unit_rows(queries.reshape(TOKENS, HK, DK)) * DK ** (-0.5), group_size, axis=1)
    keys = jnp.repeat(unit_rows(keys.reshape(TOKENS, HK, DK)), group_size, axis=1)
    values = values.reshape(TOKENS, HV, DV)
    gate_log = -decay_rate * jax.nn.softplus(a_proj + dt_bias)
    write_rate = jax.nn.sigmoid(b_proj)
    block_count = TOKENS // CH
    segment_blocks = segment.reshape(block_count, CH)
    segment_prior = jnp.concatenate([jnp.full((1,), -1, jnp.int32), segment_blocks[:-1, -1]])

    def one_head(members):
        head_q, head_k, head_v, head_g, head_b = members
        terms = block_terms(head_q.reshape(block_count, CH, DK), head_k.reshape(block_count, CH, DK), head_v.reshape(block_count, CH, DV), head_g.reshape(block_count, CH), head_b.reshape(block_count, CH), segment_blocks, segment_prior)
        _, emitted = lax.scan(advance, jnp.zeros((DK, DV), jnp.float32), terms)
        return emitted.reshape(TOKENS, DV)
    per_head = lax.map(one_head, (queries.transpose(1, 0, 2), keys.transpose(1, 0, 2), values.transpose(1, 0, 2), gate_log.T, write_rate.T))
    attended = per_head.transpose(1, 0, 2)
    gated = gated_norm(attended, z_in, norm_gain).astype(jnp.bfloat16).reshape(TOKENS, HV * DV)
    return jnp.dot(gated, out_weight, preferred_element_type=jnp.float32).astype(jnp.bfloat16)
```

```python
import jax
import jax.numpy as jnp
from jax import lax
from jax.experimental import pallas as pl
from jax.experimental.pallas import tpu as pltpu
from jax.sharding import PartitionSpec as P

DK = 128
HALO = 16
MESH = pl.DeviceIdType.MESH
f32 = jnp.float32
bf16 = jnp.bfloat16


def dot(left, right):
    return jnp.dot(left, right, preferred_element_type=f32)


def dot_t(left, right):
    return lax.dot_general(left, right, (((1,), (1,)), ((), ())), preferred_element_type=f32)


def silu(u):
    return u / (1.0 + jnp.exp(-u))


def iotas(rows, cols):
    return (
        lax.broadcasted_iota(jnp.int32, (rows, cols), 0),
        lax.broadcasted_iota(jnp.int32, (rows, cols), 1),
    )


def layer_kernel(
    n_ctx,
    n_head,
    doc,
    rate,
    dtb,
    tok,
    wq_h,
    wk_h,
    wv_h,
    wz_h,
    wa_h,
    wb_h,
    cq_h,
    ck_h,
    cv_h,
    gain_h,
    wo_h,
    out,
    xg,
    wall,
    wz,
    wa,
    wb,
    wo,
    conv,
    gain,
    acc,
    zbuf,
    eq,
    mm,
    taps,
    neg,
    cmask,
    kvb,
    abuf,
    pbuf,
    wub,
    to_s,
    to_r,
    och_s,
    och_r,
    se_s,
    sin_r,
    tchip,
    ochip,
    s_use,
    obuf,
    rbuf,
    osum,
    load_sem,
    halo_send,
    halo_recv,
    ag_send,
    ag_recv,
    to_send,
    to_recv,
    och_send,
    och_recv,
    se_send,
    sin_recv,
    rs_send,
    rs_recv,
):
    rows = tok.shape[0]
    feat = tok.shape[1]
    heads = 4
    i = lax.axis_index("ctx")
    j = lax.axis_index("head")
    core = lax.rem(i, 2)

    def ctx_at(step):
        return lax.rem(i + step + n_ctx, n_ctx)

    def head_at(step):
        return lax.rem(j + step + n_head, n_head)

    right, left, diag = head_at(1), head_at(-1), head_at(2)

    loads = [
        (tok, xg.at[j, pl.ds(HALO, rows), :]),
        (wk_h, wall.at[:, pl.ds(256, 256)]),
        (wv_h, wall.at[:, pl.ds(512, 512)]),
        (wq_h, wall.at[:, pl.ds(0, 256)]),
        (wa_h, wa),
        (wb_h, wb),
        (cq_h, conv.at[:, pl.ds(0, 256)]),
        (ck_h, conv.at[:, pl.ds(256, 256)]),
        (cv_h, conv.at[:, pl.ds(512, 512)]),
        (wz_h, wz),
        (wo_h, wo),
        (gain_h, gain),
    ]
    loads = [
        pltpu.make_async_copy(src, dst, load_sem.at[n]) for n, (src, dst) in enumerate(loads)
    ]
    for copy in loads:
        copy.start()

    barrier = pltpu.get_barrier_semaphore()
    peers = [(i, head_at(d)) for d in (1, 2, 3)]
    peers += [(ctx_at(-1), head_at(d)) for d in range(4)]
    peers += [(ctx_at(-2), j)]
    for peer in peers:
        pl.semaphore_signal(barrier, inc=1, device_id=peer, device_id_type=MESH)
    pl.semaphore_wait(barrier, len(peers))

    def remote(src, dst, send, recv, to):
        return pltpu.make_async_remote_copy(
            src_ref=src, dst_ref=dst, send_sem=send, recv_sem=recv, device_id=to, device_id_type=MESH
        )

    half = rows // 2
    lo, hi = pl.ds(HALO, half), pl.ds(HALO + half, half)
    tok_lo, tok_hi = tok.at[pl.ds(0, half), :], tok.at[pl.ds(half, half), :]
    halo = [
        remote(
            tok.at[pl.ds(rows - HALO, HALO), :],
            xg.at[j, pl.ds(0, HALO), :],
            halo_send.at[d],
            halo_recv.at[d],
            (ctx_at(1), head_at(d)),
        )
        for d in range(4)
    ]
    ring = [
        remote(tok_lo, xg.at[j, lo, :], ag_send.at[0], ag_recv.at[0], (i, right)),
        remote(tok_hi, xg.at[j, hi, :], ag_send.at[1], ag_recv.at[1], (i, right)),
        remote(tok_hi, xg.at[j, hi, :], ag_send.at[2], ag_recv.at[2], (i, left)),
        remote(tok_lo, xg.at[j, lo, :], ag_send.at[3], ag_recv.at[3], (i, left)),
        remote(xg.at[left, lo, :], xg.at[left, lo, :], ag_send.at[4], ag_recv.at[4], (i, right)),
        remote(xg.at[right, hi, :], xg.at[right, hi, :], ag_send.at[5], ag_recv.at[5], (i, left)),
    ]
    for copy in halo:
        copy.start()
    ring[0].start()
    ring[2].start()
    ring[1].start()
    ring[3].start()

    row_id, col_id = iotas(256, 256)

    def same(size):
        return (row_id // size == col_id // size).astype(f32)

    levels = [same(size) for size in (8, 16, 32, 64, 128)] + [jnp.ones((256, 256), f32)]
    mm[0] = jnp.where(row_id > col_id, levels[0], 0.0).astype(bf16)
    for n in range(5):
        mm[n + 1] = (levels[n + 1] - levels[n]).astype(bf16)
    for n in range(4):
        eq[n] = levels[n + 1].astype(bf16)
    eq[4] = (row_id >= col_id).astype(bf16)

    first = i * rows
    pos = first + lax.broadcasted_iota(jnp.int32, (8, 256), 1)

    def doc_step(n, carry):
        start, found = carry
        found = jnp.where(pos >= start, start, found)
        return start + doc[n], found

    _, found = lax.fori_loop(0, doc.shape[0], doc_step, (jnp.int32(0), jnp.zeros((8, 256), jnp.int32)))
    start_row = (found - first).astype(f32)
    start_col = jnp.broadcast_to(start_row[0:1, :], (128, 256)).T
    row_f = lax.broadcasted_iota(jnp.int32, (256, 128), 0).astype(f32)
    col_f = lax.broadcasted_iota(jnp.int32, (256, 128), 1).astype(f32)
    for n in range(3):
        taps[n] = jnp.where(row_f - (3 - n) >= start_col, 1.0, 0.0)
    for n in range(2):
        col_n = col_f + 128.0 * n
        neg[:, 128 * n : 128 * n + 128] = jnp.where(
            (col_n <= row_f) & (col_n >= start_col), 0.0, -1e30
        )
    cmask[...] = jnp.where(start_col < 0.0, 1.0, 0.0)

    lane = lax.broadcasted_iota(jnp.int32, (1, 128), 1)
    rate_row = jnp.zeros((1, 128), f32)
    dt_row = jnp.zeros((1, 128), f32)
    for h in range(heads):
        rate_row = jnp.where(lane == h, rate[h], rate_row)
        dt_row = jnp.where(lane == h, dtb[h], dt_row)

    for copy in loads[:6]:
        copy.wait()
    wall[:, 1024:1152] = jnp.concatenate(
        [wa[...], wb[...], jnp.zeros((wa.shape[0], 120), bf16)], axis=1
    )

    def slice_dot(slot):
        weights = wall[pl.ds(pl.multiple_of(slot * feat, feat), feat), :]
        return dot(xg[slot], weights)

    for copy in halo:
        copy.wait_recv()
    acc[...] = slice_dot(j)
    ring[0].wait_recv()
    ring[4].start()
    ring[2].wait_recv()
    ring[5].start()
    ring[1].wait_recv()
    acc[...] += slice_dot(left)
    ring[3].wait_recv()
    acc[...] += slice_dot(right)
    ring[4].wait_recv()
    ring[5].wait_recv()
    acc[...] += slice_dot(diag)
    acc[:, 0:1024] = acc[:, 0:1024].astype(bf16).astype(f32)

    ab = acc[HALO:, 1024:1152]
    pre = ab + dt_row
    gate = -rate_row * (jnp.maximum(pre, 0.0) + jnp.log1p(jnp.exp(-jnp.abs(pre))))
    beta = 1.0 / (1.0 + jnp.exp(-ab))
    g1 = gate.astype(bf16)
    g2 = (gate - g1.astype(f32)).astype(bf16)
    g3 = (gate - g1.astype(f32) - g2.astype(f32)).astype(bf16)
    tri = eq[4]
    cum = dot(tri, g1) + dot(tri, g2) + dot(tri, g3)
    cum_row = cum.T
    carried = jnp.exp(cum) * cmask[...]

    for copy in loads[6:9]:
        copy.wait()

    def short_conv(col):
        cols = slice(col, col + 128)
        total = acc[HALO:, cols] * conv[3:4, cols]
        for n in range(3):
            total += acc[HALO - 3 + n : HALO - 3 + n + rows, cols] * conv[n : n + 1, cols] * taps[n]
        return silu(total)

    def unit(matrix):
        return matrix * lax.rsqrt(jnp.sum(matrix * matrix, axis=-1, keepdims=True) + 1e-06)

    k_unit = [unit(short_conv(256 + 128 * n)) for n in range(2)]
    k_bf = [k.astype(bf16) for k in k_unit]
    k_dots = [dot_t(k, k) for k in k_bf]
    k_trans = [k.T for k in k_unit]
    q_unit = [unit(short_conv(128 * n)) * (DK**-0.5) for n in range(2)]
    q_dots = [dot_t(q_unit[n].astype(bf16), k_bf[n]) for n in range(2)]

    last_rows = []
    for h in range(heads):
        kh = h // 2
        decay = jnp.exp(cum[:, h : h + 1] - cum_row[h : h + 1, :] + neg[...])
        b_col = beta[:, 4 + h : 5 + h]
        abuf[h] = (k_dots[kh] * decay * b_col).astype(bf16)
        pbuf[h] = (q_dots[kh] * decay).astype(bf16)
        last_rows.append(decay[rows - 1 : rows, :])
        kvb[h, :, 0:128] = (k_unit[kh] * (b_col * carried[:, h : h + 1])).astype(bf16)
        kvb[h, :, 128:256] = (short_conv(512 + 128 * h) * b_col).astype(bf16)

    def expand(compact, level):
        size = compact.shape[0]
        return jnp.concatenate([compact.astype(bf16)] * (256 // size), axis=0) * eq[level]

    row16, col16 = iotas(16, 256)
    eye16 = (row16 == col16 % 16).astype(f32)
    every = range(heads)
    a8 = [abuf[h] * mm[0] for h in every]
    a8c = [sum(a8[h][16 * n : 16 * n + 16, :].astype(f32) for n in range(16)) for h in every]
    p2 = [dot(a8c[h].astype(bf16), a8[h]) for h in every]
    p2f = [expand(p2[h], 0) for h in every]
    x1 = [eye16 - a8c[h] for h in every]
    x2 = [x1[h] + dot(x1[h].astype(bf16), p2f[h]) for h in every]
    p4 = [dot(p2[h].astype(bf16), p2f[h]) for h in every]
    p4f = [expand(p4[h], 0) for h in every]
    d = [x2[h] + dot(x2[h].astype(bf16), p4f[h]) for h in every]
    y = [dot(d[h].astype(bf16), abuf[h] * mm[1]) for h in every]
    d = [d[h] - dot(y[h].astype(bf16), expand(d[h], 0)) for h in every]
    for n, size in enumerate((16, 32, 64, 128)):
        odd = (lax.broadcasted_iota(jnp.int32, (1, 256), 1) // size) % 2 == 1
        y = [dot(d[h].astype(bf16), abuf[h] * mm[n + 2]) for h in every]
        z = [dot(y[h].astype(bf16), expand(d[h], n)) for h in every]
        d = [
            jnp.concatenate([jnp.where(odd, 0.0, d[h]), jnp.where(odd, d[h], 0.0) - z[h]], axis=0)
            for h in every
        ]
    for h in every:
        wub[h] = dot(d[h].astype(bf16), kvb[h]).astype(bf16)

    row_k, col_k = iotas(128, 128)
    for h in every:
        k_last = (k_trans[h // 2] * last_rows[h]).astype(bf16)
        step = dot(k_last, wub[h])
        passed = jnp.where(row_k == col_k, carried[rows - 1 : rows, h : h + 1], 0.0)
        to_s[h, :, 0:128] = (passed - step[:, 0:128]).astype(bf16)
        to_s[h, :, 128:256] = step[:, 128:256].astype(bf16)

    to_copy = [
        remote(to_s.at[h], to_r.at[h], to_send.at[h], to_recv.at[h], (ctx_at(1), j)) for h in every
    ]
    och_copy = [
        remote(och_s.at[h], och_r.at[h], och_send.at[h], och_recv.at[h], (ctx_at(2), j))
        for h in every
    ]
    se_copy = [
        [
            remote(se_s.at[h], sin_r.at[h], se_send.at[n, h], sin_recv.at[h], (ctx_at(n + 1), j))
            for n in range(2)
        ]
        for h in every
    ]

    @pl.when(core == 0)
    def _():
        for copy in to_copy:
            copy.start()

    reader, local = [], []
    for h in every:
        seen = dot(pbuf[h], wub[h])
        reader.append((q_unit[h // 2] * carried[:, h : h + 1] - seen[:, 0:128]).astype(bf16))
        local.append(seen[:, 128:256])

    @pl.when(core == 1)
    def _():
        for h in every:
            to_copy[h].wait_recv()
            both = dot(to_s[h, :, 0:128], to_r[h])
            tchip[h] = both[:, 0:128].astype(bf16)
            total = both[:, 128:256] + to_s[h, :, 128:256].astype(f32)
            ochip[h] = total
            och_s[h] = total.astype(bf16)
            och_copy[h].start()

    loads[9].wait()
    z_in = jnp.zeros((rows, 512), f32)
    for n in range(4):
        z_in += dot(xg[n, HALO:, :], wz[feat * n : feat * n + feat, :])
    loads[11].wait()
    gain_row = gain[...].reshape(1, 128)
    z_in = silu(z_in.astype(bf16).astype(f32))
    for h in every:
        zbuf[:, 128 * h : 128 * h + 128] = z_in[:, 128 * h : 128 * h + 128] * gain_row

    @pl.when(core == 1)
    def _():
        for h in every:
            och_copy[h].wait_recv()
            se_s[h] = (dot(tchip[h], och_r[h]) + ochip[h]).astype(bf16)
            for copy in se_copy[h]:
                copy.start()

    loads[10].wait()

    for h in every:
        se_copy[h][0].wait_recv()

    @pl.when(core == 0)
    def _():
        s_use[...] = sin_r[...]

    @pl.when(core == 1)
    def _():
        for h in every:
            s_use[h] = (
                dot(to_r[h, :, 0:128], sin_r[h]) + to_r[h, :, 128:256].astype(f32)
            ).astype(bf16)

    gated = []
    for h in every:
        attended = dot(reader[h], s_use[h]) + local[h]
        scale = lax.rsqrt(jnp.mean(attended * attended, axis=-1, keepdims=True) + 1e-06)
        gated.append((attended * scale * zbuf[:, 128 * h : 128 * h + 128]).astype(bf16))
    gated = jnp.concatenate(gated, axis=1)

    def part(slot):
        return dot(gated, wo[:, pl.ds(pl.multiple_of(slot * feat, feat), feat)])

    rs_copy = []
    for n, step in enumerate((2, 1, 3)):
        slot = head_at(step)
        obuf[n] = part(slot).astype(bf16)
        copy = remote(obuf.at[n], rbuf.at[n], rs_send.at[n], rs_recv.at[n], (i, slot))
        copy.start()
        rs_copy.append(copy)
    osum[...] = part(j)
    for copy in rs_copy:
        copy.wait_recv()
    out[...] = (
        osum[...] + rbuf[0].astype(f32) + rbuf[1].astype(f32) + rbuf[2].astype(f32)
    ).astype(bf16)

    for copy in halo + ring + rs_copy:
        copy.wait_send()

    @pl.when(core == 0)
    def _():
        for copy in to_copy:
            copy.wait_send()

    @pl.when(core == 1)
    def _():
        for copy in och_copy:
            copy.wait_send()
        for pair in se_copy:
            for copy in pair:
                copy.wait_send()


def body(n_ctx, n_head, *arrays):
    (
        tokens,
        q_weight,
        k_weight,
        v_weight,
        z_weight,
        a_weight,
        b_weight,
        conv_q,
        conv_k,
        conv_v,
        decay_rate,
        dt_bias,
        norm_gain,
        out_weight,
        doc_lengths,
    ) = arrays
    rows, feat = tokens.shape
    smem = pl.BlockSpec(memory_space=pltpu.SMEM)
    hbm = pl.BlockSpec(memory_space=pl.ANY)
    vmem = pltpu.VMEM
    dma = pltpu.SemaphoreType.DMA
    return pl.pallas_call(
        lambda *refs: layer_kernel(n_ctx, n_head, *refs),
        out_shape=jax.ShapeDtypeStruct((rows, feat), bf16),
        in_specs=[smem] * 3 + [hbm] * 12,
        out_specs=pl.BlockSpec(memory_space=pltpu.VMEM),
        scratch_shapes=[
            vmem((4, HALO + rows, feat), bf16),
            vmem((1024, 1152), bf16),
            vmem((1024, 512), bf16),
            vmem((1024, 4), bf16),
            vmem((1024, 4), bf16),
            vmem((512, 1024), bf16),
            vmem((4, 1024), f32),
            vmem((128,), f32),
            vmem((HALO + rows, 1152), f32),
            vmem((rows, 512), f32),
            vmem((5, 256, 256), bf16),
            vmem((6, 256, 256), bf16),
            vmem((3, 256, 128), f32),
            vmem((256, 256), f32),
            vmem((256, 128), f32),
            vmem((4, 256, 256), bf16),
            vmem((4, 256, 256), bf16),
            vmem((4, 256, 256), bf16),
            vmem((4, 256, 256), bf16),
            vmem((4, 128, 256), bf16),
            vmem((4, 128, 256), bf16),
            vmem((4, 128, 128), bf16),
            vmem((4, 128, 128), bf16),
            vmem((4, 128, 128), bf16),
            vmem((4, 128, 128), bf16),
            vmem((4, 128, 128), bf16),
            vmem((4, 128, 128), f32),
            vmem((4, 128, 128), bf16),
            vmem((3, rows, feat), bf16),
            vmem((3, rows, feat), bf16),
            vmem((rows, feat), f32),
            dma((12,)),
            dma((4,)),
            dma((4,)),
            dma((6,)),
            dma((6,)),
            dma((4,)),
            dma((4,)),
            dma((4,)),
            dma((4,)),
            dma((2, 4)),
            dma((4,)),
            dma((3,)),
            dma((3,)),
        ],
        compiler_params=pltpu.CompilerParams(
            collective_id=0, has_side_effects=True, vmem_limit_bytes=48 * 1024 * 1024
        ),
        name="delta_layer",
    )(
        doc_lengths,
        decay_rate,
        dt_bias,
        tokens,
        q_weight,
        k_weight,
        v_weight,
        z_weight,
        a_weight,
        b_weight,
        conv_q,
        conv_k,
        conv_v,
        norm_gain,
        out_weight,
    )


def solution(mesh):
    n_ctx, n_head = mesh.shape["ctx"], mesh.shape["head"]
    return jax.shard_map(
        lambda *arrays: body(n_ctx, n_head, *arrays),
        mesh=mesh,
        in_specs=(
            P("ctx", "head"),
            P(None, "head"),
            P(None, "head"),
            P(None, "head"),
            P(None, "head"),
            P(None, "head"),
            P(None, "head"),
            P(None, "head"),
            P(None, "head"),
            P(None, "head"),
            P("head"),
            P("head"),
            P(),
            P("head", None),
            P(),
        ),
        out_specs=P("ctx", "head"),
        check_vma=False,
    )
```

```python
import jax
import jax.numpy as jnp
from jax import lax
from jax.experimental import pallas as pl
from jax.experimental.pallas import tpu as pltpu
from jax.sharding import PartitionSpec as P

DK = 128
HALO = 16
MESH = pl.DeviceIdType.MESH
f32 = jnp.float32
bf16 = jnp.bfloat16


def dot(left, right):
    return jnp.dot(left, right, preferred_element_type=f32)


def dot_t(left, right):
    return lax.dot_general(left, right, (((1,), (1,)), ((), ())), preferred_element_type=f32)


def silu(u):
    return u / (1.0 + jnp.exp(-u))


def iotas(rows, cols):
    return (
        lax.broadcasted_iota(jnp.int32, (rows, cols), 0),
        lax.broadcasted_iota(jnp.int32, (rows, cols), 1),
    )


def layer_kernel(
    n_ctx,
    n_head,
    doc_h,
    rate_h,
    dtb_h,
    tok,
    wq_h,
    wk_h,
    wv_h,
    wz_h,
    wa_h,
    wb_h,
    cq_h,
    ck_h,
    cv_h,
    gain_h,
    wo_h,
    out,
    doc,
    rate,
    dtb,
    xg,
    wall,
    wz,
    wab,
    wo,
    conv,
    gain,
    acc,
    zbuf,
    eq,
    mm,
    taps,
    neg,
    cmask,
    kvb,
    abuf,
    wub,
    reader,
    local,
    to_s,
    pair,
    chip_s,
    chip_r,
    off_s,
    off_r,
    use_s,
    s_use,
    obuf,
    rbuf,
    osum,
    load_sem,
    halo_send,
    halo_recv,
    ag_send,
    ag_recv,
    to_send,
    to_recv,
    chip_send,
    chip_recv,
    off_send,
    off_recv,
    use_send,
    use_recv,
    rs_send,
    rs_recv,
):
    rows = tok.shape[0]
    feat = tok.shape[1]
    heads = 4
    every = range(heads)
    i = lax.axis_index("ctx")
    j = lax.axis_index("head")
    core = lax.rem(i, 2)

    def ctx_at(step):
        return lax.rem(i + step + n_ctx, n_ctx)

    def head_at(step):
        return lax.rem(j + step + n_head, n_head)

    mate = (i + 1 - 2 * core, j)

    barrier = pltpu.get_barrier_semaphore()
    peers = [(i, head_at(d)) for d in (1, 2, 3)]
    peers += [(ctx_at(-1), head_at(d)) for d in every]
    peers += [(ctx_at(1), j), (ctx_at(-2), j), (ctx_at(-4), j)]
    for peer in peers:
        pl.semaphore_signal(barrier, inc=1, device_id=peer, device_id_type=MESH)

    loads = [
        (tok, xg.at[j, pl.ds(HALO, rows), :]),
        (wk_h, wall.at[:, pl.ds(0, 256)]),
        (wv_h, wall.at[:, pl.ds(256, 512)]),
        (wq_h, wall.at[:, pl.ds(896, 256)]),
        (wa_h, wab.at[0]),
        (wb_h, wab.at[1]),
        (ck_h, conv.at[:, pl.ds(0, 256)]),
        (cv_h, conv.at[:, pl.ds(256, 512)]),
        (cq_h, conv.at[:, pl.ds(768, 256)]),
        (wz_h, wz),
        (wo_h, wo),
        (gain_h, gain),
        (doc_h, doc),
        (rate_h, rate),
        (dtb_h, dtb),
    ]
    loads = [
        pltpu.make_async_copy(src, dst, load_sem.at[n]) for n, (src, dst) in enumerate(loads)
    ]
    for copy in loads:
        copy.start()

    def remote(src, dst, send, recv, to):
        return pltpu.make_async_remote_copy(
            src_ref=src, dst_ref=dst, send_sem=send, recv_sem=recv, device_id=to, device_id_type=MESH
        )

    halo = [
        remote(
            tok.at[pl.ds(rows - HALO, HALO), :],
            xg.at[j, pl.ds(0, HALO), :],
            halo_send.at[d],
            halo_recv.at[d],
            (ctx_at(1), head_at(d)),
        )
        for d in every
    ]
    gather = {
        d: remote(
            tok,
            xg.at[j, pl.ds(HALO, rows), :],
            ag_send.at[d - 1],
            ag_recv.at[d - 1],
            (i, head_at(d)),
        )
        for d in (1, 3, 2)
    }
    pl.semaphore_wait(barrier, len(peers))
    for copy in halo:
        copy.start()
    for copy in gather.values():
        copy.start()

    row_id, col_id = iotas(256, 256)
    apart = row_id ^ col_id
    levels = [(apart < size).astype(f32) for size in (8, 16, 32, 64, 128)] + [
        jnp.ones((256, 256), f32)
    ]
    mm[0] = jnp.where(row_id > col_id, levels[0], 0.0).astype(bf16)
    for n in range(5):
        mm[n + 1] = (levels[n + 1] - levels[n]).astype(bf16)
    for n in range(4):
        eq[n] = levels[n + 1].astype(bf16)
    eq[4] = jnp.where(row_id >= col_id, 1.0, 0.0).astype(bf16)

    for copy in loads[12:]:
        copy.wait()
    first = i * rows
    pos = first + lax.broadcasted_iota(jnp.int32, (8, 256), 1)

    def doc_step(n, carry):
        start, found = carry
        found = jnp.where(pos >= start, start, found)
        return start + doc[n], found

    _, found = lax.fori_loop(
        0, doc.shape[0], doc_step, (jnp.int32(0), jnp.zeros((8, 256), jnp.int32)), unroll=8
    )
    start_row = (found - first).astype(f32)
    start_col = jnp.broadcast_to(start_row[0:1, :], (128, 256)).T
    row_f = lax.broadcasted_iota(jnp.int32, (256, 128), 0).astype(f32)
    col_f = lax.broadcasted_iota(jnp.int32, (256, 128), 1).astype(f32)
    for n in range(3):
        taps[n] = jnp.where(row_f - (3 - n) >= start_col, 1.0, 0.0)
    for n in range(2):
        col_n = col_f + 128.0 * n
        neg[:, 128 * n : 128 * n + 128] = jnp.where(
            (col_n <= row_f) & (col_n >= start_col), 0.0, -1e30
        )
    cmask[...] = jnp.where(start_col < 0.0, 1.0, 0.0)

    lane = lax.broadcasted_iota(jnp.int32, (1, 128), 1)
    rate_row = jnp.zeros((1, 128), f32)
    dt_row = jnp.zeros((1, 128), f32)
    for h in every:
        rate_row = jnp.where(lane == h, rate[h], rate_row)
        dt_row = jnp.where(lane == h, dtb[h], dt_row)

    for copy in loads[:9]:
        copy.wait()
    wab_t = jnp.concatenate(
        [wab[0].astype(f32), wab[1].astype(f32), jnp.zeros((120, wab.shape[2]), f32)], axis=0
    )
    wall[:, 768:896] = wab_t.T.astype(bf16)

    def slice_dot(slot, begin, end):
        weights = wall[pl.ds(pl.multiple_of(slot * feat, feat), feat), begin:end]
        return dot(xg[slot], weights)

    def rounded(value):
        return value.astype(bf16).astype(f32)

    for copy in halo:
        copy.wait_recv()
    acc[...] = slice_dot(j, 0, 1152)
    gather[1].wait_recv()
    acc[...] += slice_dot(head_at(-1), 0, 1152)
    gather[3].wait_recv()
    acc[...] += slice_dot(head_at(1), 0, 1152)
    gather[2].wait_recv()
    acc[:, 768:896] += slice_dot(head_at(2), 768, 896)
    acc[:, 0:256] = rounded(acc[:, 0:256] + slice_dot(head_at(2), 0, 256))
    acc[:, 256:768] = rounded(acc[:, 256:768] + slice_dot(head_at(2), 256, 768))

    ab = acc[HALO:, 768:896]
    pre = ab + dt_row
    gate = -rate_row * (jnp.maximum(pre, 0.0) + jnp.log1p(jnp.exp(-jnp.abs(pre))))
    beta = 1.0 / (1.0 + jnp.exp(-ab))
    g1 = gate.astype(bf16)
    g2 = (gate - g1.astype(f32)).astype(bf16)
    g3 = (gate - g1.astype(f32) - g2.astype(f32)).astype(bf16)
    tri = eq[4]
    cum = dot(tri, g1) + dot(tri, g2) + dot(tri, g3)
    cum_row = cum.T
    carried = jnp.exp(cum) * cmask[...]

    def short_conv(col, tap):
        cols = slice(col, col + 128)
        weights = conv[:, tap : tap + 128]
        total = acc[HALO:, cols] * weights[3:4]
        for n in range(3):
            total += acc[HALO - 3 + n : HALO - 3 + n + rows, cols] * weights[n : n + 1] * taps[n]
        return silu(total)

    def unit(matrix):
        return matrix * lax.rsqrt(jnp.sum(matrix * matrix, axis=-1, keepdims=True) + 1e-06)

    def decay_of(h):
        return jnp.exp(cum[:, h : h + 1] - cum_row[h : h + 1, :] + neg[...])

    k_unit = [unit(short_conv(128 * n, 128 * n)) for n in range(2)]
    k_bf = [k.astype(bf16) for k in k_unit]
    k_dots = [dot_t(k, k) for k in k_bf]
    k_trans = [k.T for k in k_unit]
    last_rows = []
    for h in every:
        kh = h // 2
        decay = decay_of(h)
        b_col = beta[:, 4 + h : 5 + h]
        abuf[h] = (k_dots[kh] * decay * b_col).astype(bf16)
        last_rows.append(decay[rows - 1 : rows, :])
        kvb[h, :, 0:128] = (k_unit[kh] * (b_col * carried[:, h : h + 1])).astype(bf16)
        kvb[h, :, 128:256] = (short_conv(256 + 128 * h, 256 + 128 * h) * b_col).astype(bf16)

    def expand(compact, level):
        size = compact.shape[0]
        return jnp.concatenate([compact.astype(bf16)] * (256 // size), axis=0) * eq[level]

    row16, col16 = iotas(16, 256)
    eye16 = (row16 == (col16 & 15)).astype(f32)
    a8 = [abuf[h] * mm[0] for h in every]
    a8c = [sum(a8[h][16 * n : 16 * n + 16, :].astype(f32) for n in range(16)) for h in every]
    p2 = [dot(a8c[h].astype(bf16), a8[h]) for h in every]
    p2f = [expand(p2[h], 0) for h in every]
    x1 = [eye16 - a8c[h] for h in every]
    x2 = [x1[h] + dot(x1[h].astype(bf16), p2f[h]) for h in every]
    p4 = [dot(p2[h].astype(bf16), p2f[h]) for h in every]
    p4f = [expand(p4[h], 0) for h in every]
    d = [x2[h] + dot(x2[h].astype(bf16), p4f[h]) for h in every]
    y = [dot(d[h].astype(bf16), abuf[h] * mm[1]) for h in every]
    d = [d[h] - dot(y[h].astype(bf16), expand(d[h], 0)) for h in every]
    for n, size in enumerate((16, 32, 64, 128)):
        odd = (lax.broadcasted_iota(jnp.int32, (1, 256), 1) & size) != 0
        y = [dot(d[h].astype(bf16), abuf[h] * mm[n + 2]) for h in every]
        z = [dot(y[h].astype(bf16), expand(d[h], n)) for h in every]
        d = [
            jnp.concatenate([jnp.where(odd, 0.0, d[h]), jnp.where(odd, d[h], 0.0) - z[h]], axis=0)
            for h in every
        ]
    for h in every:
        wub[h] = dot(d[h].astype(bf16), kvb[h]).astype(bf16)

    row_k, col_k = iotas(128, 128)
    for h in every:
        k_last = (k_trans[h // 2] * last_rows[h]).astype(bf16)
        step = dot(k_last, wub[h])
        passed = jnp.where(row_k == col_k, carried[rows - 1 : rows, h : h + 1], 0.0)
        to_s[h, :, 0:128] = (passed - step[:, 0:128]).astype(bf16)
        to_s[h, :, 128:256] = step[:, 128:256].astype(bf16)

    to_copy = [
        remote(to_s.at[2 - 2 * core + n], pair.at[core, n], to_send.at[n], to_recv.at[n], mate)
        for n in range(2)
    ]
    for copy in to_copy:
        copy.start()
    for n in range(2):
        pair[core, n] = to_s[2 * core + n]
    next_copy, after_copy = [], []
    for n in range(2):
        to_copy[n].wait_recv()
        both = dot(pair[1, n, :, 0:128], pair[0, n])
        chip_s[n, :, 0:128] = both[:, 0:128].astype(bf16)
        offset = (both[:, 128:256] + pair[1, n, :, 128:256].astype(f32)).astype(bf16)
        chip_s[n, :, 128:256] = offset
        off_s[n] = offset
        after_copy.append(
            remote(off_s.at[n], off_r.at[n], off_send.at[n], off_recv.at[n], (ctx_at(4), j))
        )
        next_copy.append(
            remote(chip_s.at[n], chip_r.at[n], chip_send.at[n], chip_recv.at[n], (ctx_at(2), j))
        )
        after_copy[n].start()
        next_copy[n].start()

    q_cols = slice(896, 1152)
    acc[:, q_cols] = rounded(acc[:, q_cols] + slice_dot(head_at(2), 896, 1152))
    q_unit = [unit(short_conv(896 + 128 * n, 768 + 128 * n)) * (DK**-0.5) for n in range(2)]
    q_dots = [dot_t(q_unit[n].astype(bf16), k_bf[n]) for n in range(2)]
    for h in every:
        seen = dot((q_dots[h // 2] * decay_of(h)).astype(bf16), wub[h])
        reader[h] = (q_unit[h // 2] * carried[:, h : h + 1] - seen[:, 0:128]).astype(bf16)
        local[h] = seen[:, 128:256]

    for copy in loads[9:12]:
        copy.wait()
    z_in = jnp.zeros((rows, 512), f32)
    for n in range(4):
        z_in += dot(xg[n, HALO:, :], wz[feat * n : feat * n + feat, :])
    gain_row = gain[...].reshape(1, 128)
    z_in = silu(rounded(z_in))
    for h in every:
        zbuf[:, 128 * h : 128 * h + 128] = z_in[:, 128 * h : 128 * h + 128] * gain_row

    use_copy = [
        remote(use_s.at[n], s_use.at[2 * core + n], use_send.at[n], use_recv.at[n], mate)
        for n in range(2)
    ]
    first_core = core == 0
    for n in range(2):
        after_copy[n].wait_recv()
        next_copy[n].wait_recv()
        s_in = dot(chip_r[n, :, 0:128], off_r[n]) + chip_r[n, :, 128:256].astype(f32)
        s_mid = dot(pair[0, n, :, 0:128], s_in.astype(bf16)) + pair[0, n, :, 128:256].astype(f32)
        use_s[n] = jnp.where(first_core, s_mid, s_in).astype(bf16)
        use_copy[n].start()
        s_use[2 * core + n] = jnp.where(first_core, s_in, s_mid).astype(bf16)
    for copy in use_copy:
        copy.wait_recv()

    chunk = rows // 2
    rs_copy = []
    for c in range(2):
        span = slice(chunk * c, chunk * c + chunk)
        gated = []
        for h in every:
            attended = dot(reader[h, span, :], s_use[h]) + local[h, span, :]
            scale = lax.rsqrt(jnp.mean(attended * attended, axis=-1, keepdims=True) + 1e-06)
            gated.append((attended * scale * zbuf[span, 128 * h : 128 * h + 128]).astype(bf16))
        gated = jnp.concatenate(gated, axis=1)
        for n, d_step in enumerate((2, 1, 3)):
            slot = head_at(d_step)
            weights = wo[:, pl.ds(pl.multiple_of(slot * feat, feat), feat)]
            obuf[n, span, :] = dot(gated, weights).astype(bf16)
            copy = remote(
                obuf.at[n, pl.ds(chunk * c, chunk), :],
                rbuf.at[n, pl.ds(chunk * c, chunk), :],
                rs_send.at[c, n],
                rs_recv.at[c, n],
                (i, slot),
            )
            copy.start()
            rs_copy.append(copy)
        osum[span, :] = dot(gated, wo[:, pl.ds(pl.multiple_of(j * feat, feat), feat)])
    for c in range(2):
        span = slice(chunk * c, chunk * c + chunk)
        for copy in rs_copy[3 * c : 3 * c + 3]:
            copy.wait_recv()
        total = osum[span, :]
        for n in range(3):
            total += rbuf[n, span, :].astype(f32)
        out[span, :] = total.astype(bf16)

    gathers = [gather[d] for d in (1, 3, 2)]
    for copy in halo + gathers + to_copy + next_copy + after_copy + use_copy + rs_copy:
        copy.wait_send()


def body(n_ctx, n_head, *arrays):
    (
        tokens,
        q_weight,
        k_weight,
        v_weight,
        z_weight,
        a_weight,
        b_weight,
        conv_q,
        conv_k,
        conv_v,
        decay_rate,
        dt_bias,
        norm_gain,
        out_weight,
        doc_lengths,
    ) = arrays
    rows, feat = tokens.shape
    hbm = pl.BlockSpec(memory_space=pltpu.HBM)
    vmem = pltpu.VMEM
    dma = pltpu.SemaphoreType.DMA
    return pl.pallas_call(
        lambda *refs: layer_kernel(n_ctx, n_head, *refs),
        out_shape=jax.ShapeDtypeStruct((rows, feat), bf16),
        in_specs=[hbm] * 15,
        out_specs=pl.BlockSpec(memory_space=pltpu.VMEM),
        scratch_shapes=[
            pltpu.SMEM((64,), jnp.int32),
            pltpu.SMEM((4,), f32),
            pltpu.SMEM((4,), f32),
            vmem((4, HALO + rows, feat), bf16),
            vmem((1024, 1152), bf16),
            vmem((1024, 512), bf16),
            vmem((2, 4, 1024), bf16),
            vmem((512, 1024), bf16),
            vmem((4, 1024), f32),
            vmem((128,), f32),
            vmem((HALO + rows, 1152), f32),
            vmem((rows, 512), f32),
            vmem((5, 256, 256), bf16),
            vmem((6, 256, 256), bf16),
            vmem((3, 256, 128), f32),
            vmem((256, 256), f32),
            vmem((256, 128), f32),
            vmem((4, 256, 256), bf16),
            vmem((4, 256, 256), bf16),
            vmem((4, 256, 256), bf16),
            vmem((4, 256, 128), bf16),
            vmem((4, 256, 128), f32),
            vmem((4, 128, 256), bf16),
            vmem((2, 2, 128, 256), bf16),
            vmem((2, 128, 256), bf16),
            vmem((2, 128, 256), bf16),
            vmem((2, 128, 128), bf16),
            vmem((2, 128, 128), bf16),
            vmem((2, 128, 128), bf16),
            vmem((4, 128, 128), bf16),
            vmem((3, rows, feat), bf16),
            vmem((3, rows, feat), bf16),
            vmem((rows, feat), f32),
            dma((15,)),
            dma((4,)),
            dma((4,)),
            dma((3,)),
            dma((3,)),
            dma((2,)),
            dma((2,)),
            dma((2,)),
            dma((2,)),
            dma((2,)),
            dma((2,)),
            dma((2,)),
            dma((2,)),
            dma((2, 3)),
            dma((2, 3)),
        ],
        compiler_params=pltpu.CompilerParams(
            collective_id=0, has_side_effects=True, vmem_limit_bytes=60 * 1024 * 1024
        ),
        name="delta_layer",
    )(
        doc_lengths,
        decay_rate,
        dt_bias,
        tokens,
        q_weight,
        k_weight,
        v_weight,
        z_weight,
        a_weight.T,
        b_weight.T,
        conv_q,
        conv_k,
        conv_v,
        norm_gain,
        out_weight,
    )


def solution(mesh):
    n_ctx, n_head = mesh.shape["ctx"], mesh.shape["head"]
    return jax.shard_map(
        lambda *arrays: body(n_ctx, n_head, *arrays),
        mesh=mesh,
        in_specs=(
            P("ctx", "head"),
            P(None, "head"),
            P(None, "head"),
            P(None, "head"),
            P(None, "head"),
            P(None, "head"),
            P(None, "head"),
            P(None, "head"),
            P(None, "head"),
            P(None, "head"),
            P("head"),
            P("head"),
            P(),
            P("head", None),
            P(),
        ),
        out_specs=P("ctx", "head"),
        check_vma=False,
    )
```

```python
import jax
import jax.numpy as jnp
from jax import lax
from jax.experimental import pallas as pl
from jax.experimental.pallas import tpu as pltpu
from jax.sharding import PartitionSpec as P

DK = 128
HALO = 16
MESH = pl.DeviceIdType.MESH
f32 = jnp.float32
bf16 = jnp.bfloat16


def dot(left, right):
    return jnp.dot(left, right, preferred_element_type=f32)


def dot_t(left, right):
    return lax.dot_general(left, right, (((1,), (1,)), ((), ())), preferred_element_type=f32)


def silu(u):
    return u / (1.0 + jnp.exp(-u))


def iotas(rows, cols):
    return (
        lax.broadcasted_iota(jnp.int32, (rows, cols), 0),
        lax.broadcasted_iota(jnp.int32, (rows, cols), 1),
    )


def layer_kernel(
    n_ctx,
    n_head,
    doc_h,
    rate_h,
    dtb_h,
    tok,
    wq_h,
    wk_h,
    wv_h,
    wz_h,
    wa_h,
    wb_h,
    cq_h,
    ck_h,
    cv_h,
    gain_h,
    wo_h,
    out,
    doc,
    rate,
    dtb,
    xg,
    wall,
    wz,
    wab,
    wo,
    conv,
    gain,
    acc,
    zbuf,
    eq,
    mm,
    taps,
    neg,
    cmask,
    kvb,
    abuf,
    wub,
    reader,
    local,
    to_s,
    pair,
    chip_s,
    chip_r,
    off_s,
    off_r,
    use_s,
    s_use,
    obuf,
    rbuf,
    osum,
    load_sem,
    halo_send,
    halo_recv,
    ag_send,
    ag_recv,
    to_send,
    to_recv,
    chip_send,
    chip_recv,
    off_send,
    off_recv,
    use_send,
    use_recv,
    rs_send,
    rs_recv,
):
    rows = tok.shape[0]
    feat = tok.shape[1]
    heads = 4
    every = range(heads)
    i = lax.axis_index("ctx")
    j = lax.axis_index("head")
    core = lax.rem(i, 2)

    def ctx_at(step):
        return jnp.clip(i + step, 0, n_ctx - 1)

    def there(step):
        return (i + step < n_ctx) if step > 0 else (i + step >= 0)

    def head_at(step):
        return lax.rem(j + step + n_head, n_head)

    mate = (i + 1 - 2 * core, j)

    barrier = pltpu.get_barrier_semaphore()
    def greet(*to):
        for one in to:
            pl.semaphore_signal(barrier, inc=1, device_id=one, device_id_type=MESH)

    greet(*[(i, head_at(d)) for d in (1, 2, 3)])
    pl.when(there(-1))(lambda: greet(*[(ctx_at(-1), head_at(d)) for d in every]))
    pl.when(core == 0)(lambda: greet((ctx_at(1), j)))
    pl.when(there(-2))(lambda: greet((ctx_at(-2), j)))
    pl.when(there(-4))(lambda: greet((ctx_at(-4), j)))
    expected = 3 + core + sum(
        jnp.where(there(step), number, 0) for step, number in ((1, 4), (2, 1), (4, 1))
    )

    loads = [
        (tok, xg.at[j, pl.ds(HALO, rows), :]),
        (wk_h, wall.at[:, pl.ds(0, 256)]),
        (wv_h, wall.at[:, pl.ds(256, 512)]),
        (wq_h, wall.at[:, pl.ds(896, 256)]),
        (wa_h, wab.at[0]),
        (wb_h, wab.at[1]),
        (ck_h, conv.at[:, pl.ds(0, 256)]),
        (cv_h, conv.at[:, pl.ds(256, 512)]),
        (cq_h, conv.at[:, pl.ds(768, 256)]),
        (wz_h, wz),
        (wo_h, wo),
        (gain_h, gain),
        (doc_h, doc),
        (rate_h, rate),
        (dtb_h, dtb),
    ]
    loads = [
        pltpu.make_async_copy(src, dst, load_sem.at[n]) for n, (src, dst) in enumerate(loads)
    ]
    for copy in loads:
        copy.start()

    def remote(src, dst, send, recv, to):
        return pltpu.make_async_remote_copy(
            src_ref=src, dst_ref=dst, send_sem=send, recv_sem=recv, device_id=to, device_id_type=MESH
        )

    halo = [
        remote(
            tok.at[pl.ds(rows - HALO, HALO), :],
            xg.at[j, pl.ds(0, HALO), :],
            halo_send.at[d],
            halo_recv.at[d],
            (ctx_at(1), head_at(d)),
        )
        for d in every
    ]
    gather = {
        d: remote(
            tok,
            xg.at[j, pl.ds(HALO, rows), :],
            ag_send.at[d - 1],
            ag_recv.at[d - 1],
            (i, head_at(d)),
        )
        for d in (1, 3, 2)
    }
    pl.semaphore_wait(barrier, expected)
    for copy in gather.values():
        copy.start()

    @pl.when(there(1))
    def _():
        for copy in halo:
            copy.start()


    row_id, col_id = iotas(256, 256)
    apart = row_id ^ col_id
    levels = [(apart < size).astype(f32) for size in (8, 16, 32, 64, 128)] + [
        jnp.ones((256, 256), f32)
    ]
    mm[0] = jnp.where(row_id > col_id, levels[0], 0.0).astype(bf16)
    for n in range(5):
        mm[n + 1] = (levels[n + 1] - levels[n]).astype(bf16)
    for n in range(4):
        eq[n] = levels[n + 1].astype(bf16)
    eq[4] = jnp.where(row_id >= col_id, 1.0, 0.0).astype(bf16)

    for copy in loads[12:]:
        copy.wait()
    first = i * rows
    pos = first + lax.broadcasted_iota(jnp.int32, (8, 256), 1)

    def doc_step(n, carry):
        start, found = carry
        found = jnp.where(pos >= start, start, found)
        return start + doc[n], found

    _, found = lax.fori_loop(
        0, doc.shape[0], doc_step, (jnp.int32(0), jnp.zeros((8, 256), jnp.int32)), unroll=8
    )
    start_row = (found - first).astype(f32)
    start_col = jnp.broadcast_to(start_row[0:1, :], (128, 256)).T
    row_f = lax.broadcasted_iota(jnp.int32, (256, 128), 0).astype(f32)
    col_f = lax.broadcasted_iota(jnp.int32, (256, 128), 1).astype(f32)
    for n in range(3):
        taps[n] = jnp.where(row_f - (3 - n) >= start_col, 1.0, 0.0)
    for n in range(2):
        col_n = col_f + 128.0 * n
        neg[:, 128 * n : 128 * n + 128] = jnp.where(
            (col_n <= row_f) & (col_n >= start_col), 0.0, -1e30
        )
    cmask[...] = jnp.where(start_col < 0.0, 1.0, 0.0)

    lane = lax.broadcasted_iota(jnp.int32, (1, 128), 1)
    rate_row = jnp.zeros((1, 128), f32)
    dt_row = jnp.zeros((1, 128), f32)
    for h in every:
        rate_row = jnp.where(lane == h, rate[h], rate_row)
        dt_row = jnp.where(lane == h, dtb[h], dt_row)

    for copy in loads[:9]:
        copy.wait()
    wab_t = jnp.concatenate(
        [wab[0].astype(f32), wab[1].astype(f32), jnp.zeros((120, wab.shape[2]), f32)], axis=0
    )
    wall[:, 768:896] = wab_t.T.astype(bf16)

    def slice_dot(slot, begin, end):
        weights = wall[pl.ds(pl.multiple_of(slot * feat, feat), feat), begin:end]
        return dot(xg[slot], weights)

    def rounded(value):
        return value.astype(bf16).astype(f32)

    @pl.when(there(-1))
    def _():
        for copy in halo:
            copy.wait_recv()

    @pl.when(i == 0)
    def _():
        xg[:, 0:HALO, :] = jnp.zeros((4, HALO, feat), bf16)

    acc[...] = slice_dot(j, 0, 1152)
    gather[1].wait_recv()
    acc[...] += slice_dot(head_at(-1), 0, 1152)
    gather[3].wait_recv()
    acc[...] += slice_dot(head_at(1), 0, 1152)
    gather[2].wait_recv()
    acc[:, 768:896] += slice_dot(head_at(2), 768, 896)
    acc[:, 0:256] = rounded(acc[:, 0:256] + slice_dot(head_at(2), 0, 256))
    acc[:, 256:768] = rounded(acc[:, 256:768] + slice_dot(head_at(2), 256, 768))

    ab = acc[HALO:, 768:896]
    pre = ab + dt_row
    gate = -rate_row * (jnp.maximum(pre, 0.0) + jnp.log1p(jnp.exp(-jnp.abs(pre))))
    beta = 1.0 / (1.0 + jnp.exp(-ab))
    g1 = gate.astype(bf16)
    g2 = (gate - g1.astype(f32)).astype(bf16)
    g3 = (gate - g1.astype(f32) - g2.astype(f32)).astype(bf16)
    tri = eq[4]
    cum = dot(tri, g1) + dot(tri, g2) + dot(tri, g3)
    cum_row = cum.T
    carried = jnp.exp(cum) * cmask[...]

    def short_conv(col, tap):
        cols = slice(col, col + 128)
        weights = conv[:, tap : tap + 128]
        total = acc[HALO:, cols] * weights[3:4]
        for n in range(3):
            total += acc[HALO - 3 + n : HALO - 3 + n + rows, cols] * weights[n : n + 1] * taps[n]
        return silu(total)

    def unit(matrix):
        return matrix * lax.rsqrt(jnp.sum(matrix * matrix, axis=-1, keepdims=True) + 1e-06)

    def decay_of(h):
        return jnp.exp(cum[:, h : h + 1] - cum_row[h : h + 1, :] + neg[...])

    k_unit = [unit(short_conv(128 * n, 128 * n)) for n in range(2)]
    k_bf = [k.astype(bf16) for k in k_unit]
    k_dots = [dot_t(k, k) for k in k_bf]
    k_trans = [k.T for k in k_unit]
    last_rows = []
    for h in every:
        kh = h // 2
        decay = decay_of(h)
        b_col = beta[:, 4 + h : 5 + h]
        abuf[h] = (k_dots[kh] * decay * b_col).astype(bf16)
        last_rows.append(decay[rows - 1 : rows, :])
        kvb[h, :, 0:128] = (k_unit[kh] * (b_col * carried[:, h : h + 1])).astype(bf16)
        kvb[h, :, 128:256] = (short_conv(256 + 128 * h, 256 + 128 * h) * b_col).astype(bf16)

    def expand(compact, level):
        size = compact.shape[0]
        return jnp.concatenate([compact.astype(bf16)] * (256 // size), axis=0) * eq[level]

    row16, col16 = iotas(16, 256)
    eye16 = (row16 == (col16 & 15)).astype(f32)
    a8 = [abuf[h] * mm[0] for h in every]
    a8c = [sum(a8[h][16 * n : 16 * n + 16, :].astype(f32) for n in range(16)) for h in every]
    p2 = [dot(a8c[h].astype(bf16), a8[h]) for h in every]
    p2f = [expand(p2[h], 0) for h in every]
    x1 = [eye16 - a8c[h] for h in every]
    x2 = [x1[h] + dot(x1[h].astype(bf16), p2f[h]) for h in every]
    p4 = [dot(p2[h].astype(bf16), p2f[h]) for h in every]
    p4f = [expand(p4[h], 0) for h in every]
    d = [x2[h] + dot(x2[h].astype(bf16), p4f[h]) for h in every]
    y = [dot(d[h].astype(bf16), abuf[h] * mm[1]) for h in every]
    d = [d[h] - dot(y[h].astype(bf16), expand(d[h], 0)) for h in every]
    for n, size in enumerate((16, 32, 64, 128)):
        odd = (lax.broadcasted_iota(jnp.int32, (1, 256), 1) & size) != 0
        y = [dot(d[h].astype(bf16), abuf[h] * mm[n + 2]) for h in every]
        z = [dot(y[h].astype(bf16), expand(d[h], n)) for h in every]
        d = [
            jnp.concatenate([jnp.where(odd, 0.0, d[h]), jnp.where(odd, d[h], 0.0) - z[h]], axis=0)
            for h in every
        ]
    for h in every:
        wub[h] = dot(d[h].astype(bf16), kvb[h]).astype(bf16)

    row_k, col_k = iotas(128, 128)
    for h in every:
        k_last = (k_trans[h // 2] * last_rows[h]).astype(bf16)
        step = dot(k_last, wub[h])
        passed = jnp.where(row_k == col_k, carried[rows - 1 : rows, h : h + 1], 0.0)
        to_s[h, :, 0:128] = (passed - step[:, 0:128]).astype(bf16)
        to_s[h, :, 128:256] = step[:, 128:256].astype(bf16)

    to_copy = [
        remote(to_s.at[2 - 2 * core + n], pair.at[core, n], to_send.at[n], to_recv.at[n], mate)
        for n in range(2)
    ]
    for copy in to_copy:
        copy.start()
    for n in range(2):
        pair[core, n] = to_s[2 * core + n]
    next_copy, after_copy = [], []
    for n in range(2):
        to_copy[n].wait_recv()
        both = dot(pair[1, n, :, 0:128], pair[0, n])
        chip_s[n, :, 0:128] = both[:, 0:128].astype(bf16)
        offset = (both[:, 128:256] + pair[1, n, :, 128:256].astype(f32)).astype(bf16)
        chip_s[n, :, 128:256] = offset
        off_s[n] = offset
        after_copy.append(
            remote(off_s.at[n], off_r.at[n], off_send.at[n], off_recv.at[n], (ctx_at(4), j))
        )
        next_copy.append(
            remote(chip_s.at[n], chip_r.at[n], chip_send.at[n], chip_recv.at[n], (ctx_at(2), j))
        )
        pl.when(there(4))(after_copy[n].start)
        pl.when(there(2))(next_copy[n].start)

    q_cols = slice(896, 1152)
    acc[:, q_cols] = rounded(acc[:, q_cols] + slice_dot(head_at(2), 896, 1152))
    q_unit = [unit(short_conv(896 + 128 * n, 768 + 128 * n)) * (DK**-0.5) for n in range(2)]
    q_dots = [dot_t(q_unit[n].astype(bf16), k_bf[n]) for n in range(2)]
    for h in every:
        seen = dot((q_dots[h // 2] * decay_of(h)).astype(bf16), wub[h])
        reader[h] = (q_unit[h // 2] * carried[:, h : h + 1] - seen[:, 0:128]).astype(bf16)
        local[h] = seen[:, 128:256]

    for copy in loads[9:12]:
        copy.wait()
    z_in = jnp.zeros((rows, 512), f32)
    for n in range(4):
        z_in += dot(xg[n, HALO:, :], wz[feat * n : feat * n + feat, :])
    gain_row = gain[...].reshape(1, 128)
    z_in = silu(rounded(z_in))
    for h in every:
        zbuf[:, 128 * h : 128 * h + 128] = z_in[:, 128 * h : 128 * h + 128] * gain_row

    use_copy = [
        remote(use_s.at[n], s_use.at[2 * core + n], use_send.at[n], use_recv.at[n], mate)
        for n in range(2)
    ]
    first_core = core == 0

    @pl.when(i < 2)
    def _():
        chip_r[...] = jnp.zeros(chip_r.shape, bf16)

    @pl.when(i < 4)
    def _():
        off_r[...] = jnp.zeros(off_r.shape, bf16)

    for n in range(2):
        pl.when(there(-4))(after_copy[n].wait_recv)
        pl.when(there(-2))(next_copy[n].wait_recv)
        s_in = dot(chip_r[n, :, 0:128], off_r[n]) + chip_r[n, :, 128:256].astype(f32)
        s_mid = dot(pair[0, n, :, 0:128], s_in.astype(bf16)) + pair[0, n, :, 128:256].astype(f32)
        use_s[n] = jnp.where(first_core, s_mid, s_in).astype(bf16)
        use_copy[n].start()
        s_use[2 * core + n] = jnp.where(first_core, s_in, s_mid).astype(bf16)
    for copy in use_copy:
        copy.wait_recv()

    chunk = rows // 2
    rs_copy = []
    for c in range(2):
        span = slice(chunk * c, chunk * c + chunk)
        gated = []
        for h in every:
            attended = dot(reader[h, span, :], s_use[h]) + local[h, span, :]
            scale = lax.rsqrt(jnp.mean(attended * attended, axis=-1, keepdims=True) + 1e-06)
            gated.append((attended * scale * zbuf[span, 128 * h : 128 * h + 128]).astype(bf16))
        gated = jnp.concatenate(gated, axis=1)
        for n, d_step in enumerate((2, 1, 3)):
            slot = head_at(d_step)
            weights = wo[:, pl.ds(pl.multiple_of(slot * feat, feat), feat)]
            obuf[n, span, :] = dot(gated, weights).astype(bf16)
            copy = remote(
                obuf.at[n, pl.ds(chunk * c, chunk), :],
                rbuf.at[n, pl.ds(chunk * c, chunk), :],
                rs_send.at[c, n],
                rs_recv.at[c, n],
                (i, slot),
            )
            copy.start()
            rs_copy.append(copy)
        osum[span, :] = dot(gated, wo[:, pl.ds(pl.multiple_of(j * feat, feat), feat)])
    for c in range(2):
        span = slice(chunk * c, chunk * c + chunk)
        for copy in rs_copy[3 * c : 3 * c + 3]:
            copy.wait_recv()
        total = osum[span, :]
        for n in range(3):
            total += rbuf[n, span, :].astype(f32)
        out[span, :] = total.astype(bf16)

    gathers = [gather[d] for d in (1, 3, 2)]
    for copy in gathers + to_copy + use_copy + rs_copy:
        copy.wait_send()
    for step, copies in ((1, halo), (2, next_copy), (4, after_copy)):

        @pl.when(there(step))
        def _(copies=copies):
            for copy in copies:
                copy.wait_send()


def body(n_ctx, n_head, *arrays):
    (
        tokens,
        q_weight,
        k_weight,
        v_weight,
        z_weight,
        a_weight,
        b_weight,
        conv_q,
        conv_k,
        conv_v,
        decay_rate,
        dt_bias,
        norm_gain,
        out_weight,
        doc_lengths,
    ) = arrays
    rows, feat = tokens.shape
    hbm = pl.BlockSpec(memory_space=pltpu.HBM)
    vmem = pltpu.VMEM
    dma = pltpu.SemaphoreType.DMA
    return pl.pallas_call(
        lambda *refs: layer_kernel(n_ctx, n_head, *refs),
        out_shape=jax.ShapeDtypeStruct((rows, feat), bf16),
        in_specs=[hbm] * 15,
        out_specs=pl.BlockSpec(memory_space=pltpu.VMEM),
        scratch_shapes=[
            pltpu.SMEM((64,), jnp.int32),
            pltpu.SMEM((4,), f32),
            pltpu.SMEM((4,), f32),
            vmem((4, HALO + rows, feat), bf16),
            vmem((1024, 1152), bf16),
            vmem((1024, 512), bf16),
            vmem((2, 4, 1024), bf16),
            vmem((512, 1024), bf16),
            vmem((4, 1024), f32),
            vmem((128,), f32),
            vmem((HALO + rows, 1152), f32),
            vmem((rows, 512), f32),
            vmem((5, 256, 256), bf16),
            vmem((6, 256, 256), bf16),
            vmem((3, 256, 128), f32),
            vmem((256, 256), f32),
            vmem((256, 128), f32),
            vmem((4, 256, 256), bf16),
            vmem((4, 256, 256), bf16),
            vmem((4, 256, 256), bf16),
            vmem((4, 256, 128), bf16),
            vmem((4, 256, 128), f32),
            vmem((4, 128, 256), bf16),
            vmem((2, 2, 128, 256), bf16),
            vmem((2, 128, 256), bf16),
            vmem((2, 128, 256), bf16),
            vmem((2, 128, 128), bf16),
            vmem((2, 128, 128), bf16),
            vmem((2, 128, 128), bf16),
            vmem((4, 128, 128), bf16),
            vmem((3, rows, feat), bf16),
            vmem((3, rows, feat), bf16),
            vmem((rows, feat), f32),
            dma((15,)),
            dma((4,)),
            dma((4,)),
            dma((3,)),
            dma((3,)),
            dma((2,)),
            dma((2,)),
            dma((2,)),
            dma((2,)),
            dma((2,)),
            dma((2,)),
            dma((2,)),
            dma((2,)),
            dma((2, 3)),
            dma((2, 3)),
        ],
        compiler_params=pltpu.CompilerParams(
            collective_id=0, has_side_effects=True, vmem_limit_bytes=60 * 1024 * 1024
        ),
        name="delta_layer",
    )(
        doc_lengths,
        decay_rate,
        dt_bias,
        tokens,
        q_weight,
        k_weight,
        v_weight,
        z_weight,
        a_weight.T,
        b_weight.T,
        conv_q,
        conv_k,
        conv_v,
        norm_gain,
        out_weight,
    )


def solution(mesh):
    n_ctx, n_head = mesh.shape["ctx"], mesh.shape["head"]
    return jax.shard_map(
        lambda *arrays: body(n_ctx, n_head, *arrays),
        mesh=mesh,
        in_specs=(
            P("ctx", "head"),
            P(None, "head"),
            P(None, "head"),
            P(None, "head"),
            P(None, "head"),
            P(None, "head"),
            P(None, "head"),
            P(None, "head"),
            P(None, "head"),
            P(None, "head"),
            P("head"),
            P("head"),
            P(),
            P("head", None),
            P(),
        ),
        out_specs=P("ctx", "head"),
        check_vma=False,
    )
```

```python
import jax
import jax.numpy as jnp
from jax import lax
from jax.experimental import pallas as pl
from jax.experimental.pallas import tpu as pltpu
from jax.sharding import PartitionSpec as P

DK = 128
HALO = 16
MESH = pl.DeviceIdType.MESH
f32 = jnp.float32
bf16 = jnp.bfloat16


def dot(left, right):
    return jnp.dot(left, right, preferred_element_type=f32)


def dot_t(left, right):
    return lax.dot_general(left, right, (((1,), (1,)), ((), ())), preferred_element_type=f32)


def silu(u):
    return (0.5 * u) * (1.0 + jnp.tanh(0.5 * u))


def iotas(rows, cols):
    return (
        lax.broadcasted_iota(jnp.int32, (rows, cols), 0),
        lax.broadcasted_iota(jnp.int32, (rows, cols), 1),
    )


def layer_kernel(
    n_ctx,
    n_head,
    doc_h,
    rate_h,
    dtb_h,
    tok,
    wq_h,
    wk_h,
    wv_h,
    wz_h,
    wa_h,
    wb_h,
    cq_h,
    ck_h,
    cv_h,
    gain_h,
    wo_h,
    out,
    doc,
    rate,
    dtb,
    xg,
    wall,
    wz,
    wab,
    wo,
    conv,
    gain,
    acc,
    zbuf,
    eq,
    mm,
    taps,
    neg,
    cmask,
    kvb,
    abuf,
    wub,
    reader,
    local,
    to_s,
    pair,
    chip_s,
    chip_r,
    off_s,
    off_r,
    use_s,
    s_use,
    obuf,
    rbuf,
    osum,
    load_sem,
    halo_send,
    halo_recv,
    ag_send,
    ag_recv,
    to_send,
    to_recv,
    chip_send,
    chip_recv,
    off_send,
    off_recv,
    use_send,
    use_recv,
    rs_send,
    rs_recv,
):
    rows = tok.shape[0]
    feat = tok.shape[1]
    heads = 4
    every = range(heads)
    i = lax.axis_index("ctx")
    j = lax.axis_index("head")
    core = lax.rem(i, 2)

    def ctx_at(step):
        return jnp.clip(i + step, 0, n_ctx - 1)

    def there(step):
        return (i + step < n_ctx) if step > 0 else (i + step >= 0)

    def head_at(step):
        return lax.rem(j + step + n_head, n_head)

    mate = (i + 1 - 2 * core, j)

    barrier = pltpu.get_barrier_semaphore()
    def greet(*to):
        for one in to:
            pl.semaphore_signal(barrier, inc=1, device_id=one, device_id_type=MESH)

    greet(*[(i, head_at(d)) for d in (1, 2, 3)])
    pl.when(there(-1))(lambda: greet(*[(ctx_at(-1), head_at(d)) for d in every]))
    pl.when(core == 0)(lambda: greet((ctx_at(1), j)))
    pl.when(there(-2))(lambda: greet((ctx_at(-2), j)))
    pl.when(there(-4))(lambda: greet((ctx_at(-4), j)))
    expected = 3 + core + sum(
        jnp.where(there(step), number, 0) for step, number in ((1, 4), (2, 1), (4, 1))
    )

    loads = [
        (tok, xg.at[j, pl.ds(HALO, rows), :]),
        (wk_h, wall.at[:, pl.ds(0, 256)]),
        (wv_h, wall.at[:, pl.ds(256, 512)]),
        (wq_h, wall.at[:, pl.ds(896, 256)]),
        (wa_h, wab.at[0]),
        (wb_h, wab.at[1]),
        (ck_h, conv.at[:, pl.ds(0, 256)]),
        (cv_h, conv.at[:, pl.ds(256, 512)]),
        (cq_h, conv.at[:, pl.ds(768, 256)]),
        (wz_h, wz),
        (wo_h, wo),
        (gain_h, gain),
        (doc_h, doc),
        (rate_h, rate),
        (dtb_h, dtb),
    ]
    loads = [
        pltpu.make_async_copy(src, dst, load_sem.at[n]) for n, (src, dst) in enumerate(loads)
    ]
    def remote(src, dst, send, recv, to):
        return pltpu.make_async_remote_copy(
            src_ref=src, dst_ref=dst, send_sem=send, recv_sem=recv, device_id=to, device_id_type=MESH
        )

    halo = [
        remote(
            tok.at[pl.ds(rows - HALO, HALO), :],
            xg.at[j, pl.ds(0, HALO), :],
            halo_send.at[d],
            halo_recv.at[d],
            (ctx_at(1), head_at(d)),
        )
        for d in every
    ]
    edge = rows // 4
    right, left = head_at(1), head_at(-1)

    def move(number, owner, begin, count, to):
        source = xg.at[owner, pl.ds(HALO + begin, count), :]
        mine = tok.at[pl.ds(begin, count), :]
        return remote(
            mine if owner is j else source, source, ag_send.at[number], ag_recv.at[number], (i, to)
        )

    gather = [
        move(0, j, 0, edge, right),
        move(1, j, rows - edge, edge, left),
        move(2, j, edge, rows - 2 * edge, head_at(2)),
        move(3, j, edge, rows - edge, right),
        move(4, j, 0, rows - edge, left),
    ]
    forward = [move(5, left, 0, edge, right), move(6, right, rows - edge, edge, left)]
    pl.semaphore_wait(barrier, expected)
    for copy in gather:
        copy.start()

    @pl.when(there(1))
    def _():
        for copy in halo:
            copy.start()

    for copy in loads:
        copy.start()

    row_id, col_id = iotas(256, 256)
    apart = row_id ^ col_id
    levels = [(apart < size).astype(f32) for size in (8, 16, 32, 64, 128)] + [
        jnp.ones((256, 256), f32)
    ]
    mm[0] = jnp.where(row_id > col_id, levels[0], 0.0).astype(bf16)
    for n in range(5):
        mm[n + 1] = (levels[n + 1] - levels[n]).astype(bf16)
    for n in range(4):
        eq[n] = levels[n + 1].astype(bf16)
    eq[4] = jnp.where(row_id >= col_id, 1.0, 0.0).astype(bf16)

    for copy in loads[12:]:
        copy.wait()
    first = i * rows
    pos = first + lax.broadcasted_iota(jnp.int32, (8, 256), 1)

    def doc_step(n, carry):
        start, found = carry
        found = jnp.where(pos >= start, start, found)
        return start + doc[n], found

    _, found = lax.fori_loop(
        0, doc.shape[0], doc_step, (jnp.int32(0), jnp.zeros((8, 256), jnp.int32)), unroll=8
    )
    start_row = (found - first).astype(f32)
    start_col = jnp.broadcast_to(start_row[0:1, :], (128, 256)).T
    row_f = lax.broadcasted_iota(jnp.int32, (256, 128), 0).astype(f32)
    col_f = lax.broadcasted_iota(jnp.int32, (256, 128), 1).astype(f32)
    for n in range(3):
        taps[n] = jnp.where(row_f - (3 - n) >= start_col, 1.0, 0.0)
    for n in range(2):
        col_n = col_f + 128.0 * n
        neg[:, 128 * n : 128 * n + 128] = jnp.where(
            (col_n <= row_f) & (col_n >= start_col), 0.0, -1e30
        )
    cmask[...] = jnp.where(start_col < 0.0, 1.0, 0.0)

    lane = lax.broadcasted_iota(jnp.int32, (1, 128), 1)
    rate_row = jnp.zeros((1, 128), f32)
    dt_row = jnp.zeros((1, 128), f32)
    for h in every:
        rate_row = jnp.where(lane == h, rate[h], rate_row)
        dt_row = jnp.where(lane == h, dtb[h], dt_row)

    for n in range(2):
        gather[n].wait_recv()
        forward[n].start()

    for copy in loads[:9]:
        copy.wait()
    wab_t = jnp.concatenate(
        [wab[0].astype(f32), wab[1].astype(f32), jnp.zeros((120, wab.shape[2]), f32)], axis=0
    )
    wall[:, 768:896] = wab_t.T.astype(bf16)

    def slice_dot(slot, begin, end):
        weights = wall[pl.ds(pl.multiple_of(slot * feat, feat), feat), begin:end]
        return dot(xg[slot], weights)

    def rounded(value):
        return value.astype(bf16).astype(f32)

    @pl.when(there(-1))
    def _():
        for copy in halo:
            copy.wait_recv()

    @pl.when(i == 0)
    def _():
        xg[:, 0:HALO, :] = jnp.zeros((4, HALO, feat), bf16)

    acc[...] = slice_dot(j, 0, 1152)
    gather[3].wait_recv()
    acc[...] += slice_dot(left, 0, 1152)
    gather[4].wait_recv()
    acc[...] += slice_dot(right, 0, 1152)
    for copy in (gather[2], forward[0], forward[1]):
        copy.wait_recv()
    acc[:, 768:896] += slice_dot(head_at(2), 768, 896)
    acc[:, 0:256] = rounded(acc[:, 0:256] + slice_dot(head_at(2), 0, 256))
    acc[:, 256:768] = rounded(acc[:, 256:768] + slice_dot(head_at(2), 256, 768))

    def short_conv(col, tap):
        cols = slice(col, col + 128)
        weights = conv[:, tap : tap + 128]
        total = acc[HALO:, cols] * weights[3:4]
        for n in range(3):
            total += acc[HALO - 3 + n : HALO - 3 + n + rows, cols] * weights[n : n + 1] * taps[n]
        return silu(total)

    def unit(matrix):
        return matrix * lax.rsqrt(jnp.sum(matrix * matrix, axis=-1, keepdims=True) + 1e-06)


    k_unit = [unit(short_conv(128 * n, 128 * n)) for n in range(2)]
    k_bf = [k.astype(bf16) for k in k_unit]
    k_dots = [dot_t(k, k) for k in k_bf]
    k_trans = [k.T for k in k_unit]
    ab = acc[HALO:, 768:896]
    pre = ab + dt_row
    gate = -rate_row * (jnp.maximum(pre, 0.0) + jnp.log1p(jnp.exp(-jnp.abs(pre))))
    beta = 1.0 / (1.0 + jnp.exp(-ab))
    g1 = gate.astype(bf16)
    g2 = (gate - g1.astype(f32)).astype(bf16)
    g3 = (gate - g1.astype(f32) - g2.astype(f32)).astype(bf16)
    tri = eq[4]
    cum = dot(tri, g1) + dot(tri, g2) + dot(tri, g3)
    cum_row = cum.T
    carried = jnp.exp(cum) * cmask[...]

    def decay_of(h):
        return jnp.exp(cum[:, h : h + 1] - cum_row[h : h + 1, :] + neg[...])

    last_rows = []
    for h in every:
        kh = h // 2
        decay = decay_of(h)
        b_col = beta[:, 4 + h : 5 + h]
        abuf[h] = (k_dots[kh] * decay * b_col).astype(bf16)
        last_rows.append(decay[rows - 1 : rows, :])
        kvb[h, :, 0:128] = (k_unit[kh] * (b_col * carried[:, h : h + 1])).astype(bf16)
        kvb[h, :, 128:256] = (short_conv(256 + 128 * h, 256 + 128 * h) * b_col).astype(bf16)

    def expand(compact, level):
        size = compact.shape[0]
        return jnp.concatenate([compact.astype(bf16)] * (256 // size), axis=0) * eq[level]

    row16, col16 = iotas(16, 256)
    eye16 = (row16 == (col16 & 15)).astype(f32)
    a8 = [abuf[h] * mm[0] for h in every]
    a8c = [sum(a8[h][16 * n : 16 * n + 16, :] for n in range(1, 16)) + a8[h][0:16, :] for h in every]
    p2 = [dot(a8c[h], a8[h]) for h in every]
    p2f = [expand(p2[h], 0) for h in every]
    x1 = [eye16 - a8c[h].astype(f32) for h in every]
    x2 = [x1[h] + dot(x1[h].astype(bf16), p2f[h]) for h in every]
    p4 = [dot(p2[h].astype(bf16), p2f[h]) for h in every]
    p4f = [expand(p4[h], 0) for h in every]
    d = [x2[h] + dot(x2[h].astype(bf16), p4f[h]) for h in every]
    y = [dot(d[h].astype(bf16), abuf[h] * mm[1]) for h in every]
    d = [d[h] - dot(y[h].astype(bf16), expand(d[h], 0)) for h in every]
    for n, size in enumerate((16, 32, 64)):
        odd = (lax.broadcasted_iota(jnp.int32, (1, 256), 1) & size) != 0
        y = [dot(d[h].astype(bf16), abuf[h] * mm[n + 2]) for h in every]
        z = [dot(y[h].astype(bf16), expand(d[h], n)) for h in every]
        d = [
            jnp.concatenate([jnp.where(odd, 0.0, d[h]), jnp.where(odd, d[h], 0.0) - z[h]], axis=0)
            for h in every
        ]
    upper = [d[h][:, 0:128].astype(bf16) for h in every]
    lower = [d[h][:, 128:256].astype(bf16) for h in every]
    x_up = [dot(upper[h], kvb[h, 0:128, :]).astype(bf16) for h in every]
    y = [dot(lower[h], abuf[h, 128:256, 0:128]).astype(bf16) for h in every]
    x_low = [dot(lower[h], kvb[h, 128:256, :]) for h in every]
    for h in every:
        wub[h, 0:128, :] = x_up[h]
        wub[h, 128:256, :] = (x_low[h] - dot(y[h], x_up[h])).astype(bf16)

    row_k, col_k = iotas(128, 128)
    for h in every:
        k_last = (k_trans[h // 2] * last_rows[h]).astype(bf16)
        step = dot(k_last, wub[h])
        passed = jnp.where(row_k == col_k, carried[rows - 1 : rows, h : h + 1], 0.0)
        to_s[h, :, 0:128] = (passed - step[:, 0:128]).astype(bf16)
        to_s[h, :, 128:256] = step[:, 128:256].astype(bf16)

    to_copy = [
        remote(to_s.at[2 - 2 * core + n], pair.at[core, n], to_send.at[n], to_recv.at[n], mate)
        for n in range(2)
    ]
    for copy in to_copy:
        copy.start()
    for n in range(2):
        pair[core, n] = to_s[2 * core + n]
    next_copy, after_copy = [], []
    for n in range(2):
        to_copy[n].wait_recv()
        both = dot(pair[1, n, :, 0:128], pair[0, n])
        chip_s[n, :, 0:128] = both[:, 0:128].astype(bf16)
        offset = (both[:, 128:256] + pair[1, n, :, 128:256].astype(f32)).astype(bf16)
        chip_s[n, :, 128:256] = offset
        off_s[n] = offset
        after_copy.append(
            remote(off_s.at[n], off_r.at[n], off_send.at[n], off_recv.at[n], (ctx_at(4), j))
        )
        next_copy.append(
            remote(chip_s.at[n], chip_r.at[n], chip_send.at[n], chip_recv.at[n], (ctx_at(2), j))
        )
        pl.when(there(4))(after_copy[n].start)
        pl.when(there(2))(next_copy[n].start)

    q_cols = slice(896, 1152)
    acc[:, q_cols] = rounded(acc[:, q_cols] + slice_dot(head_at(2), 896, 1152))
    q_unit = [unit(short_conv(896 + 128 * n, 768 + 128 * n)) * (DK**-0.5) for n in range(2)]
    q_dots = [dot_t(q_unit[n].astype(bf16), k_bf[n]) for n in range(2)]
    for h in every:
        seen = dot((q_dots[h // 2] * decay_of(h)).astype(bf16), wub[h])
        reader[h] = (q_unit[h // 2] * carried[:, h : h + 1] - seen[:, 0:128]).astype(bf16)
        local[h] = seen[:, 128:256]

    for copy in loads[9:12]:
        copy.wait()
    z_in = jnp.zeros((rows, 512), f32)
    for n in range(4):
        z_in += dot(xg[n, HALO:, :], wz[feat * n : feat * n + feat, :])
    gain_row = gain[...].reshape(1, 128)
    z_in = silu(rounded(z_in))
    for h in every:
        zbuf[:, 128 * h : 128 * h + 128] = z_in[:, 128 * h : 128 * h + 128] * gain_row

    use_copy = [
        remote(use_s.at[n], s_use.at[2 * core + n], use_send.at[n], use_recv.at[n], mate)
        for n in range(2)
    ]
    first_core = core == 0

    @pl.when(i < 2)
    def _():
        chip_r[...] = jnp.zeros(chip_r.shape, bf16)

    @pl.when(i < 4)
    def _():
        off_r[...] = jnp.zeros(off_r.shape, bf16)

    for n in range(2):
        pl.when(there(-4))(after_copy[n].wait_recv)
        pl.when(there(-2))(next_copy[n].wait_recv)
        s_in = dot(chip_r[n, :, 0:128], off_r[n]) + chip_r[n, :, 128:256].astype(f32)
        s_mid = dot(pair[0, n, :, 0:128], s_in.astype(bf16)) + pair[0, n, :, 128:256].astype(f32)
        use_s[n] = jnp.where(first_core, s_mid, s_in).astype(bf16)
        use_copy[n].start()
        s_use[2 * core + n] = jnp.where(first_core, s_in, s_mid).astype(bf16)
    for copy in use_copy:
        copy.wait_recv()

    chunks = 4
    chunk = rows // chunks
    rs_copy = []
    for c in range(chunks):
        span = slice(chunk * c, chunk * c + chunk)
        gated = []
        for h in every:
            attended = dot(reader[h, span, :], s_use[h]) + local[h, span, :]
            scale = lax.rsqrt(jnp.mean(attended * attended, axis=-1, keepdims=True) + 1e-06)
            gated.append((attended * scale * zbuf[span, 128 * h : 128 * h + 128]).astype(bf16))
        gated = jnp.concatenate(gated, axis=1)
        for n, d_step in enumerate((2, 1, 3)):
            slot = head_at(d_step)
            weights = wo[:, pl.ds(pl.multiple_of(slot * feat, feat), feat)]
            obuf[n, span, :] = dot(gated, weights).astype(bf16)
            copy = remote(
                obuf.at[n, pl.ds(chunk * c, chunk), :],
                rbuf.at[n, pl.ds(chunk * c, chunk), :],
                rs_send.at[c, n],
                rs_recv.at[c, n],
                (i, slot),
            )
            copy.start()
            rs_copy.append(copy)
        osum[span, :] = dot(gated, wo[:, pl.ds(pl.multiple_of(j * feat, feat), feat)])
    for c in range(chunks):
        span = slice(chunk * c, chunk * c + chunk)
        for copy in rs_copy[3 * c : 3 * c + 3]:
            copy.wait_recv()
        total = osum[span, :]
        for n in range(3):
            total += rbuf[n, span, :].astype(f32)
        out[span, :] = total.astype(bf16)

    gathers = gather + forward
    for copy in gathers + to_copy + use_copy + rs_copy:
        copy.wait_send()
    for step, copies in ((1, halo), (2, next_copy), (4, after_copy)):

        @pl.when(there(step))
        def _(copies=copies):
            for copy in copies:
                copy.wait_send()


def body(n_ctx, n_head, *arrays):
    (
        tokens,
        q_weight,
        k_weight,
        v_weight,
        z_weight,
        a_weight,
        b_weight,
        conv_q,
        conv_k,
        conv_v,
        decay_rate,
        dt_bias,
        norm_gain,
        out_weight,
        doc_lengths,
    ) = arrays
    rows, feat = tokens.shape
    hbm = pl.BlockSpec(memory_space=pltpu.HBM)
    vmem = pltpu.VMEM
    dma = pltpu.SemaphoreType.DMA
    return pl.pallas_call(
        lambda *refs: layer_kernel(n_ctx, n_head, *refs),
        out_shape=jax.ShapeDtypeStruct((rows, feat), bf16),
        in_specs=[hbm] * 15,
        out_specs=pl.BlockSpec(memory_space=pltpu.VMEM),
        scratch_shapes=[
            pltpu.SMEM((64,), jnp.int32),
            pltpu.SMEM((4,), f32),
            pltpu.SMEM((4,), f32),
            vmem((4, HALO + rows, feat), bf16),
            vmem((1024, 1152), bf16),
            vmem((1024, 512), bf16),
            vmem((2, 4, 1024), bf16),
            vmem((512, 1024), bf16),
            vmem((4, 1024), f32),
            vmem((128,), f32),
            vmem((HALO + rows, 1152), f32),
            vmem((rows, 512), f32),
            vmem((5, 256, 256), bf16),
            vmem((6, 256, 256), bf16),
            vmem((3, 256, 128), f32),
            vmem((256, 256), f32),
            vmem((256, 128), f32),
            vmem((4, 256, 256), bf16),
            vmem((4, 256, 256), bf16),
            vmem((4, 256, 256), bf16),
            vmem((4, 256, 128), bf16),
            vmem((4, 256, 128), f32),
            vmem((4, 128, 256), bf16),
            vmem((2, 2, 128, 256), bf16),
            vmem((2, 128, 256), bf16),
            vmem((2, 128, 256), bf16),
            vmem((2, 128, 128), bf16),
            vmem((2, 128, 128), bf16),
            vmem((2, 128, 128), bf16),
            vmem((4, 128, 128), bf16),
            vmem((3, rows, feat), bf16),
            vmem((3, rows, feat), bf16),
            vmem((rows, feat), f32),
            dma((15,)),
            dma((4,)),
            dma((4,)),
            dma((7,)),
            dma((7,)),
            dma((2,)),
            dma((2,)),
            dma((2,)),
            dma((2,)),
            dma((2,)),
            dma((2,)),
            dma((2,)),
            dma((2,)),
            dma((4, 3)),
            dma((4, 3)),
        ],
        compiler_params=pltpu.CompilerParams(
            collective_id=0, has_side_effects=True, vmem_limit_bytes=60 * 1024 * 1024
        ),
        name="delta_layer",
    )(
        doc_lengths,
        decay_rate,
        dt_bias,
        tokens,
        q_weight,
        k_weight,
        v_weight,
        z_weight,
        a_weight.T,
        b_weight.T,
        conv_q,
        conv_k,
        conv_v,
        norm_gain,
        out_weight,
    )


def solution(mesh):
    n_ctx, n_head = mesh.shape["ctx"], mesh.shape["head"]
    return jax.shard_map(
        lambda *arrays: body(n_ctx, n_head, *arrays),
        mesh=mesh,
        in_specs=(
            P("ctx", "head"),
            P(None, "head"),
            P(None, "head"),
            P(None, "head"),
            P(None, "head"),
            P(None, "head"),
            P(None, "head"),
            P(None, "head"),
            P(None, "head"),
            P(None, "head"),
            P("head"),
            P("head"),
            P(),
            P("head", None),
            P(),
        ),
        out_specs=P("ctx", "head"),
        check_vma=False,
    )
```

```python
import jax
import jax.numpy as jnp
from jax import lax
from jax.experimental import pallas as pl
from jax.experimental.pallas import tpu as pltpu
from jax.sharding import PartitionSpec as P

DK = 128
HALO = 16
MESH = pl.DeviceIdType.MESH
f32 = jnp.float32
bf16 = jnp.bfloat16


def dot(left, right):
    return jnp.dot(left, right, preferred_element_type=f32)


def dot_t(left, right):
    return lax.dot_general(left, right, (((1,), (1,)), ((), ())), preferred_element_type=f32)


def silu(u):
    return (0.5 * u) * (1.0 + jnp.tanh(0.5 * u))


def iotas(rows, cols):
    return (
        lax.broadcasted_iota(jnp.int32, (rows, cols), 0),
        lax.broadcasted_iota(jnp.int32, (rows, cols), 1),
    )


def layer_kernel(
    n_ctx,
    n_head,
    doc_h,
    rate_h,
    dtb_h,
    tok,
    wq_h,
    wk_h,
    wv_h,
    wz_h,
    wa_h,
    wb_h,
    cq_h,
    ck_h,
    cv_h,
    gain_h,
    wo_h,
    out,
    doc,
    rate,
    dtb,
    xg,
    wall,
    wz,
    wab,
    wo,
    conv,
    gain,
    acc,
    zbuf,
    eq,
    mm,
    taps,
    neg,
    cmask,
    kvb,
    abuf,
    wub,
    reader,
    local,
    to_s,
    pair,
    chip_s,
    chip_r,
    off_s,
    off_r,
    use_s,
    s_use,
    obuf,
    rbuf,
    osum,
    load_sem,
    halo_send,
    halo_recv,
    ag_send,
    ag_recv,
    to_send,
    to_recv,
    chip_send,
    chip_recv,
    off_send,
    off_recv,
    use_send,
    use_recv,
    rs_send,
    rs_recv,
    ready,
):
    rows = tok.shape[0]
    feat = tok.shape[1]
    heads = 4
    every = range(heads)
    i = lax.axis_index("ctx")
    j = lax.axis_index("head")
    core = lax.rem(i, 2)

    def ctx_at(step):
        return jnp.clip(i + step, 0, n_ctx - 1)

    def there(step):
        return (i + step < n_ctx) if step > 0 else (i + step >= 0)

    def head_at(step):
        return lax.rem(j + step + n_head, n_head)

    mate = (i + 1 - 2 * core, j)

    barrier = pltpu.get_barrier_semaphore()
    def tell(semaphore, to):
        pl.semaphore_signal(semaphore, inc=1, device_id=to, device_id_type=MESH)

    for d in (1, 2, 3):
        tell(barrier, (i, head_at(d)))
    pl.when(there(1))(lambda: tell(barrier, (ctx_at(1), j)))
    pl.when(there(-1))(lambda: tell(barrier, (ctx_at(-1), j)))
    expected = 3 + jnp.where(there(1), 1, 0) + jnp.where(there(-1), 1, 0)

    def pass_on(level):
        pl.when(there(level + 1) & there(-1))(lambda: tell(ready.at[level], (ctx_at(-1), j)))

    def hear(level):
        pl.when(there(level + 2))(lambda: pl.semaphore_wait(ready.at[level], 1))

    loads = [
        (tok, xg.at[j, pl.ds(HALO, rows), :]),
        (wk_h, wall.at[:, pl.ds(0, 256)]),
        (wv_h, wall.at[:, pl.ds(256, 512)]),
        (wq_h, wall.at[:, pl.ds(896, 256)]),
        (wa_h, wab.at[0]),
        (wb_h, wab.at[1]),
        (ck_h, conv.at[:, pl.ds(0, 256)]),
        (cv_h, conv.at[:, pl.ds(256, 512)]),
        (cq_h, conv.at[:, pl.ds(768, 256)]),
        (wz_h, wz),
        (wo_h, wo),
        (gain_h, gain),
        (doc_h, doc),
        (rate_h, rate),
        (dtb_h, dtb),
    ]
    loads = [
        pltpu.make_async_copy(src, dst, load_sem.at[n]) for n, (src, dst) in enumerate(loads)
    ]
    def remote(src, dst, send, recv, to):
        return pltpu.make_async_remote_copy(
            src_ref=src, dst_ref=dst, send_sem=send, recv_sem=recv, device_id=to, device_id_type=MESH
        )

    first_rows = pl.ds(0, HALO)
    halo = remote(
        tok.at[pl.ds(rows - HALO, HALO), :],
        xg.at[j, first_rows, :],
        halo_send.at[0],
        halo_recv.at[0],
        (ctx_at(1), j),
    )
    halo_on = [
        remote(
            xg.at[j, first_rows, :],
            xg.at[j, first_rows, :],
            halo_send.at[d],
            halo_recv.at[d],
            (i, head_at(d)),
        )
        for d in (2, 1, 3)
    ]
    edge = rows // 4
    right, left = head_at(1), head_at(-1)

    def move(number, owner, begin, count, to):
        source = xg.at[owner, pl.ds(HALO + begin, count), :]
        mine = tok.at[pl.ds(begin, count), :]
        return remote(
            mine if owner is j else source, source, ag_send.at[number], ag_recv.at[number], (i, to)
        )

    gather = [
        move(0, j, 0, edge, right),
        move(1, j, rows - edge, edge, left),
        move(2, j, edge, rows - 2 * edge, head_at(2)),
        move(3, j, edge, rows - edge, right),
        move(4, j, 0, rows - edge, left),
    ]
    forward = [move(5, left, 0, edge, right), move(6, right, rows - edge, edge, left)]
    pl.semaphore_wait(barrier, expected)
    pl.when(there(1))(halo.start)
    for copy in gather:
        copy.start()
    pass_on(0)
    for copy in loads:
        copy.start()

    row_id, col_id = iotas(256, 256)
    apart = row_id ^ col_id
    levels = [(apart < size).astype(f32) for size in (8, 16, 32, 64, 128)] + [
        jnp.ones((256, 256), f32)
    ]
    mm[0] = jnp.where(row_id > col_id, levels[0], 0.0).astype(bf16)
    for n in range(5):
        mm[n + 1] = (levels[n + 1] - levels[n]).astype(bf16)
    for n in range(4):
        eq[n] = levels[n + 1].astype(bf16)
    eq[4] = jnp.where(row_id >= col_id, 1.0, 0.0).astype(bf16)

    for copy in loads[12:]:
        copy.wait()
    first = i * rows
    pos = first + lax.broadcasted_iota(jnp.int32, (8, 256), 1)

    def doc_step(n, carry):
        start, found = carry
        found = jnp.where(pos >= start, start, found)
        return start + doc[n], found

    _, found = lax.fori_loop(
        0, doc.shape[0], doc_step, (jnp.int32(0), jnp.zeros((8, 256), jnp.int32)), unroll=8
    )
    start_row = (found - first).astype(f32)
    start_col = jnp.broadcast_to(start_row[0:1, :], (128, 256)).T
    row_f = lax.broadcasted_iota(jnp.int32, (256, 128), 0).astype(f32)
    col_f = lax.broadcasted_iota(jnp.int32, (256, 128), 1).astype(f32)
    for n in range(3):
        taps[n] = jnp.where(row_f - (3 - n) >= start_col, 1.0, 0.0)
    for n in range(2):
        col_n = col_f + 128.0 * n
        neg[:, 128 * n : 128 * n + 128] = jnp.where(
            (col_n <= row_f) & (col_n >= start_col), 0.0, -1e30
        )
    cmask[...] = jnp.where(start_col < 0.0, 1.0, 0.0)

    lane = lax.broadcasted_iota(jnp.int32, (1, 128), 1)
    rate_row = jnp.zeros((1, 128), f32)
    dt_row = jnp.zeros((1, 128), f32)
    for h in every:
        rate_row = jnp.where(lane == h, rate[h], rate_row)
        dt_row = jnp.where(lane == h, dtb[h], dt_row)

    for n in range(2):
        gather[n].wait_recv()
        forward[n].start()

    @pl.when(there(-1))
    def _():
        halo.wait_recv()
        for copy in halo_on:
            copy.start()

    @pl.when(i == 0)
    def _():
        xg[:, 0:HALO, :] = jnp.zeros((4, HALO, feat), bf16)

    hear(0)
    pass_on(1)

    for copy in loads[:9]:
        copy.wait()
    wab_t = jnp.concatenate(
        [wab[0].astype(f32), wab[1].astype(f32), jnp.zeros((120, wab.shape[2]), f32)], axis=0
    )
    wall[:, 768:896] = wab_t.T.astype(bf16)

    def slice_dot(slot, begin, end):
        weights = wall[pl.ds(pl.multiple_of(slot * feat, feat), feat), begin:end]
        return dot(xg[slot], weights)

    def rounded(value):
        return value.astype(bf16).astype(f32)

    acc[...] = slice_dot(j, 0, 1152)
    hear(1)
    pass_on(2)
    @pl.when(there(-1))
    def _():
        for copy in halo_on:
            copy.wait_recv()

    gather[3].wait_recv()
    acc[...] += slice_dot(left, 0, 1152)
    gather[4].wait_recv()
    acc[...] += slice_dot(right, 0, 1152)
    for copy in (gather[2], forward[0], forward[1]):
        copy.wait_recv()
    acc[:, 768:896] += slice_dot(head_at(2), 768, 896)
    acc[:, 0:256] = rounded(acc[:, 0:256] + slice_dot(head_at(2), 0, 256))
    acc[:, 256:768] = rounded(acc[:, 256:768] + slice_dot(head_at(2), 256, 768))

    def short_conv(col, tap):
        cols = slice(col, col + 128)
        weights = conv[:, tap : tap + 128]
        total = acc[HALO:, cols] * weights[3:4]
        for n in range(3):
            total += acc[HALO - 3 + n : HALO - 3 + n + rows, cols] * weights[n : n + 1] * taps[n]
        return silu(total)

    def unit(matrix):
        return matrix * lax.rsqrt(jnp.sum(matrix * matrix, axis=-1, keepdims=True) + 1e-06)


    k_unit = [unit(short_conv(128 * n, 128 * n)) for n in range(2)]
    k_bf = [k.astype(bf16) for k in k_unit]
    k_dots = [dot_t(k, k) for k in k_bf]
    k_trans = [k.T for k in k_unit]
    ab = acc[HALO:, 768:896]
    pre = ab + dt_row
    gate = -rate_row * (jnp.maximum(pre, 0.0) + jnp.log1p(jnp.exp(-jnp.abs(pre))))
    beta = 1.0 / (1.0 + jnp.exp(-ab))
    g1 = gate.astype(bf16)
    g2 = (gate - g1.astype(f32)).astype(bf16)
    g3 = (gate - g1.astype(f32) - g2.astype(f32)).astype(bf16)
    tri = eq[4]
    cum = dot(tri, g1) + dot(tri, g2) + dot(tri, g3)
    cum_row = cum.T
    carried = jnp.exp(cum) * cmask[...]

    def decay_of(h):
        return jnp.exp(cum[:, h : h + 1] - cum_row[h : h + 1, :] + neg[...])

    last_rows = []
    for h in every:
        kh = h // 2
        decay = decay_of(h)
        b_col = beta[:, 4 + h : 5 + h]
        abuf[h] = (k_dots[kh] * decay * b_col).astype(bf16)
        last_rows.append(decay[rows - 1 : rows, :])
        kvb[h, :, 0:128] = (k_unit[kh] * (b_col * carried[:, h : h + 1])).astype(bf16)
        kvb[h, :, 128:256] = (short_conv(256 + 128 * h, 256 + 128 * h) * b_col).astype(bf16)

    def expand(compact, level):
        size = compact.shape[0]
        return jnp.concatenate([compact.astype(bf16)] * (256 // size), axis=0) * eq[level]

    row16, col16 = iotas(16, 256)
    eye16 = (row16 == (col16 & 15)).astype(f32)
    a8 = [abuf[h] * mm[0] for h in every]
    a8c = [sum(a8[h][16 * n : 16 * n + 16, :] for n in range(1, 16)) + a8[h][0:16, :] for h in every]
    p2 = [dot(a8c[h], a8[h]) for h in every]
    p2f = [expand(p2[h], 0) for h in every]
    x1 = [eye16 - a8c[h].astype(f32) for h in every]
    x2 = [x1[h] + dot(x1[h].astype(bf16), p2f[h]) for h in every]
    p4 = [dot(p2[h].astype(bf16), p2f[h]) for h in every]
    p4f = [expand(p4[h], 0) for h in every]
    d = [x2[h] + dot(x2[h].astype(bf16), p4f[h]) for h in every]
    y = [dot(d[h].astype(bf16), abuf[h] * mm[1]) for h in every]
    d = [d[h] - dot(y[h].astype(bf16), expand(d[h], 0)) for h in every]
    for n, size in enumerate((16, 32, 64)):
        odd = (lax.broadcasted_iota(jnp.int32, (1, 256), 1) & size) != 0
        y = [dot(d[h].astype(bf16), abuf[h] * mm[n + 2]) for h in every]
        z = [dot(y[h].astype(bf16), expand(d[h], n)) for h in every]
        d = [
            jnp.concatenate([jnp.where(odd, 0.0, d[h]), jnp.where(odd, d[h], 0.0) - z[h]], axis=0)
            for h in every
        ]
    upper = [d[h][:, 0:128].astype(bf16) for h in every]
    lower = [d[h][:, 128:256].astype(bf16) for h in every]
    x_up = [dot(upper[h], kvb[h, 0:128, :]).astype(bf16) for h in every]
    y = [dot(lower[h], abuf[h, 128:256, 0:128]).astype(bf16) for h in every]
    x_low = [dot(lower[h], kvb[h, 128:256, :]) for h in every]
    for h in every:
        wub[h, 0:128, :] = x_up[h]
        wub[h, 128:256, :] = (x_low[h] - dot(y[h], x_up[h])).astype(bf16)

    row_k, col_k = iotas(128, 128)
    for h in every:
        k_last = (k_trans[h // 2] * last_rows[h]).astype(bf16)
        step = dot(k_last, wub[h])
        passed = jnp.where(row_k == col_k, carried[rows - 1 : rows, h : h + 1], 0.0)
        to_s[h, :, 0:128] = (passed - step[:, 0:128]).astype(bf16)
        to_s[h, :, 128:256] = step[:, 128:256].astype(bf16)

    hear(2)
    to_copy = [
        remote(to_s.at[2 - 2 * core + n], pair.at[core, n], to_send.at[n], to_recv.at[n], mate)
        for n in range(2)
    ]
    for copy in to_copy:
        copy.start()
    for n in range(2):
        pair[core, n] = to_s[2 * core + n]
    next_copy, after_copy = [], []
    for n in range(2):
        to_copy[n].wait_recv()
        both = dot(pair[1, n, :, 0:128], pair[0, n])
        chip_s[n, :, 0:128] = both[:, 0:128].astype(bf16)
        offset = (both[:, 128:256] + pair[1, n, :, 128:256].astype(f32)).astype(bf16)
        chip_s[n, :, 128:256] = offset
        off_s[n] = offset
        after_copy.append(
            remote(off_s.at[n], off_r.at[n], off_send.at[n], off_recv.at[n], (ctx_at(4), j))
        )
        next_copy.append(
            remote(chip_s.at[n], chip_r.at[n], chip_send.at[n], chip_recv.at[n], (ctx_at(2), j))
        )
        pl.when(there(4))(after_copy[n].start)
        pl.when(there(2))(next_copy[n].start)

    q_cols = slice(896, 1152)
    acc[:, q_cols] = rounded(acc[:, q_cols] + slice_dot(head_at(2), 896, 1152))
    q_unit = [unit(short_conv(896 + 128 * n, 768 + 128 * n)) * (DK**-0.5) for n in range(2)]
    q_dots = [dot_t(q_unit[n].astype(bf16), k_bf[n]) for n in range(2)]
    for h in every:
        seen = dot((q_dots[h // 2] * decay_of(h)).astype(bf16), wub[h])
        reader[h] = (q_unit[h // 2] * carried[:, h : h + 1] - seen[:, 0:128]).astype(bf16)
        local[h] = seen[:, 128:256]

    for copy in loads[9:12]:
        copy.wait()
    z_in = jnp.zeros((rows, 512), f32)
    for n in range(4):
        z_in += dot(xg[n, HALO:, :], wz[feat * n : feat * n + feat, :])
    gain_row = gain[...].reshape(1, 128)
    z_in = silu(rounded(z_in))
    for h in every:
        zbuf[:, 128 * h : 128 * h + 128] = z_in[:, 128 * h : 128 * h + 128] * gain_row

    use_copy = [
        remote(use_s.at[n], s_use.at[2 * core + n], use_send.at[n], use_recv.at[n], mate)
        for n in range(2)
    ]
    first_core = core == 0

    @pl.when(i < 2)
    def _():
        chip_r[...] = jnp.zeros(chip_r.shape, bf16)

    @pl.when(i < 4)
    def _():
        off_r[...] = jnp.zeros(off_r.shape, bf16)

    for n in range(2):
        pl.when(there(-4))(after_copy[n].wait_recv)
        pl.when(there(-2))(next_copy[n].wait_recv)
        s_in = dot(chip_r[n, :, 0:128], off_r[n]) + chip_r[n, :, 128:256].astype(f32)
        s_mid = dot(pair[0, n, :, 0:128], s_in.astype(bf16)) + pair[0, n, :, 128:256].astype(f32)
        use_s[n] = jnp.where(first_core, s_mid, s_in).astype(bf16)
        use_copy[n].start()
        s_use[2 * core + n] = jnp.where(first_core, s_in, s_mid).astype(bf16)
    for copy in use_copy:
        copy.wait_recv()

    chunks = 4
    chunk = rows // chunks
    rs_copy = []
    for c in range(chunks):
        span = slice(chunk * c, chunk * c + chunk)
        gated = []
        for h in every:
            attended = dot(reader[h, span, :], s_use[h]) + local[h, span, :]
            scale = lax.rsqrt(jnp.mean(attended * attended, axis=-1, keepdims=True) + 1e-06)
            gated.append((attended * scale * zbuf[span, 128 * h : 128 * h + 128]).astype(bf16))
        gated = jnp.concatenate(gated, axis=1)
        for n, d_step in enumerate((2, 1, 3)):
            slot = head_at(d_step)
            weights = wo[:, pl.ds(pl.multiple_of(slot * feat, feat), feat)]
            obuf[n, span, :] = dot(gated, weights).astype(bf16)
            copy = remote(
                obuf.at[n, pl.ds(chunk * c, chunk), :],
                rbuf.at[n, pl.ds(chunk * c, chunk), :],
                rs_send.at[c, n],
                rs_recv.at[c, n],
                (i, slot),
            )
            copy.start()
            rs_copy.append(copy)
        osum[span, :] = dot(gated, wo[:, pl.ds(pl.multiple_of(j * feat, feat), feat)])
    for c in range(chunks):
        span = slice(chunk * c, chunk * c + chunk)
        for copy in rs_copy[3 * c : 3 * c + 3]:
            copy.wait_recv()
        total = osum[span, :]
        for n in range(3):
            total += rbuf[n, span, :].astype(f32)
        out[span, :] = total.astype(bf16)

    gathers = gather + forward
    for copy in gathers + to_copy + use_copy + rs_copy:
        copy.wait_send()
    for step, copies in ((1, [halo]), (-1, halo_on), (2, next_copy), (4, after_copy)):

        @pl.when(there(step))
        def _(copies=copies):
            for copy in copies:
                copy.wait_send()


def body(n_ctx, n_head, *arrays):
    (
        tokens,
        q_weight,
        k_weight,
        v_weight,
        z_weight,
        a_weight,
        b_weight,
        conv_q,
        conv_k,
        conv_v,
        decay_rate,
        dt_bias,
        norm_gain,
        out_weight,
        doc_lengths,
    ) = arrays
    rows, feat = tokens.shape
    hbm = pl.BlockSpec(memory_space=pltpu.HBM)
    vmem = pltpu.VMEM
    dma = pltpu.SemaphoreType.DMA
    return pl.pallas_call(
        lambda *refs: layer_kernel(n_ctx, n_head, *refs),
        out_shape=jax.ShapeDtypeStruct((rows, feat), bf16),
        in_specs=[hbm] * 15,
        out_specs=pl.BlockSpec(memory_space=pltpu.VMEM),
        scratch_shapes=[
            pltpu.SMEM((64,), jnp.int32),
            pltpu.SMEM((4,), f32),
            pltpu.SMEM((4,), f32),
            vmem((4, HALO + rows, feat), bf16),
            vmem((1024, 1152), bf16),
            vmem((1024, 512), bf16),
            vmem((2, 4, 1024), bf16),
            vmem((512, 1024), bf16),
            vmem((4, 1024), f32),
            vmem((128,), f32),
            vmem((HALO + rows, 1152), f32),
            vmem((rows, 512), f32),
            vmem((5, 256, 256), bf16),
            vmem((6, 256, 256), bf16),
            vmem((3, 256, 128), f32),
            vmem((256, 256), f32),
            vmem((256, 128), f32),
            vmem((4, 256, 256), bf16),
            vmem((4, 256, 256), bf16),
            vmem((4, 256, 256), bf16),
            vmem((4, 256, 128), bf16),
            vmem((4, 256, 128), f32),
            vmem((4, 128, 256), bf16),
            vmem((2, 2, 128, 256), bf16),
            vmem((2, 128, 256), bf16),
            vmem((2, 128, 256), bf16),
            vmem((2, 128, 128), bf16),
            vmem((2, 128, 128), bf16),
            vmem((2, 128, 128), bf16),
            vmem((4, 128, 128), bf16),
            vmem((3, rows, feat), bf16),
            vmem((3, rows, feat), bf16),
            vmem((rows, feat), f32),
            dma((15,)),
            dma((4,)),
            dma((4,)),
            dma((7,)),
            dma((7,)),
            dma((2,)),
            dma((2,)),
            dma((2,)),
            dma((2,)),
            dma((2,)),
            dma((2,)),
            dma((2,)),
            dma((2,)),
            dma((4, 3)),
            dma((4, 3)),
            pltpu.SemaphoreType.REGULAR((3,)),
        ],
        compiler_params=pltpu.CompilerParams(
            collective_id=0, has_side_effects=True, vmem_limit_bytes=60 * 1024 * 1024
        ),
        name="delta_layer",
    )(
        doc_lengths,
        decay_rate,
        dt_bias,
        tokens,
        q_weight,
        k_weight,
        v_weight,
        z_weight,
        a_weight.T,
        b_weight.T,
        conv_q,
        conv_k,
        conv_v,
        norm_gain,
        out_weight,
    )


def solution(mesh):
    n_ctx, n_head = mesh.shape["ctx"], mesh.shape["head"]
    return jax.shard_map(
        lambda *arrays: body(n_ctx, n_head, *arrays),
        mesh=mesh,
        in_specs=(
            P("ctx", "head"),
            P(None, "head"),
            P(None, "head"),
            P(None, "head"),
            P(None, "head"),
            P(None, "head"),
            P(None, "head"),
            P(None, "head"),
            P(None, "head"),
            P(None, "head"),
            P("head"),
            P("head"),
            P(),
            P("head", None),
            P(),
        ),
        out_specs=P("ctx", "head"),
        check_vma=False,
    )
```

```python
import jax
import jax.numpy as jnp
from jax import lax
from jax.experimental import pallas as pl
from jax.experimental.pallas import tpu as pltpu
from jax.sharding import PartitionSpec as P

DK = 128
HALO = 16
MESH = pl.DeviceIdType.MESH
f32 = jnp.float32
bf16 = jnp.bfloat16


def dot(left, right):
    return jnp.dot(left, right, preferred_element_type=f32)


def dot_t(left, right):
    return lax.dot_general(left, right, (((1,), (1,)), ((), ())), preferred_element_type=f32)


def silu(u):
    return (0.5 * u) * (1.0 + jnp.tanh(0.5 * u))


def iotas(rows, cols):
    return (
        lax.broadcasted_iota(jnp.int32, (rows, cols), 0),
        lax.broadcasted_iota(jnp.int32, (rows, cols), 1),
    )


def layer_kernel(
    n_ctx,
    n_head,
    doc_h,
    rate_h,
    dtb_h,
    tok,
    wq_h,
    wk_h,
    wv_h,
    wz_h,
    wa_h,
    wb_h,
    cq_h,
    ck_h,
    cv_h,
    gain_h,
    wo_h,
    out,
    doc,
    rate,
    dtb,
    xg,
    wall,
    wz,
    wab,
    wo,
    conv,
    gain,
    acc,
    zbuf,
    eq,
    mm,
    taps,
    neg,
    cmask,
    kvb,
    abuf,
    wub,
    reader,
    local,
    to_s,
    pair,
    chip_s,
    chip_r,
    off_s,
    off_r,
    use_s,
    s_use,
    obuf,
    rbuf,
    osum,
    load_sem,
    halo_send,
    halo_recv,
    ag_send,
    ag_recv,
    to_send,
    to_recv,
    chip_send,
    chip_recv,
    off_send,
    off_recv,
    use_send,
    use_recv,
    rs_send,
    rs_recv,
    ready,
):
    rows = tok.shape[0]
    feat = tok.shape[1]
    heads = 4
    every = range(heads)
    i = lax.axis_index("ctx")
    j = lax.axis_index("head")
    core = lax.rem(i, 2)

    def ctx_at(step):
        return jnp.clip(i + step, 0, n_ctx - 1)

    def there(step):
        return (i + step < n_ctx) if step > 0 else (i + step >= 0)

    def head_at(step):
        return lax.rem(j + step + n_head, n_head)

    mate = (i + 1 - 2 * core, j)

    barrier = pltpu.get_barrier_semaphore()
    def tell(semaphore, to):
        pl.semaphore_signal(semaphore, inc=1, device_id=to, device_id_type=MESH)

    for d in (1, 2, 3):
        tell(barrier, (i, head_at(d)))
    pl.when(there(1))(lambda: tell(barrier, (ctx_at(1), j)))
    pl.when(there(-1))(lambda: tell(barrier, (ctx_at(-1), j)))
    expected = 3 + jnp.where(there(1), 1, 0) + jnp.where(there(-1), 1, 0)

    def pass_on(level):
        pl.when(there(level + 1) & there(-1))(lambda: tell(ready.at[level], (ctx_at(-1), j)))

    def hear(level):
        pl.when(there(level + 2))(lambda: pl.semaphore_wait(ready.at[level], 1))

    loads = [
        (tok, xg.at[j, pl.ds(HALO, rows), :]),
        (wk_h, wall.at[:, pl.ds(0, 256)]),
        (wv_h, wall.at[:, pl.ds(256, 512)]),
        (wq_h, wall.at[:, pl.ds(896, 256)]),
        (wa_h, wab.at[0]),
        (wb_h, wab.at[1]),
        (ck_h, conv.at[:, pl.ds(0, 256)]),
        (cv_h, conv.at[:, pl.ds(256, 512)]),
        (cq_h, conv.at[:, pl.ds(768, 256)]),
        (wz_h, wz),
        (wo_h, wo),
        (gain_h, gain),
        (doc_h, doc),
        (rate_h, rate),
        (dtb_h, dtb),
    ]
    loads = [
        pltpu.make_async_copy(src, dst, load_sem.at[n]) for n, (src, dst) in enumerate(loads)
    ]
    def remote(src, dst, send, recv, to):
        return pltpu.make_async_remote_copy(
            src_ref=src, dst_ref=dst, send_sem=send, recv_sem=recv, device_id=to, device_id_type=MESH
        )

    first_rows = pl.ds(0, HALO)
    halo = remote(
        tok.at[pl.ds(rows - HALO, HALO), :],
        xg.at[j, first_rows, :],
        halo_send.at[0],
        halo_recv.at[0],
        (ctx_at(1), j),
    )
    halo_on = [
        remote(
            xg.at[j, first_rows, :],
            xg.at[j, first_rows, :],
            halo_send.at[d],
            halo_recv.at[d],
            (i, head_at(d)),
        )
        for d in (2, 1, 3)
    ]
    edge = rows // 4
    right, left = head_at(1), head_at(-1)

    def move(number, owner, begin, count, to):
        source = xg.at[owner, pl.ds(HALO + begin, count), :]
        mine = tok.at[pl.ds(begin, count), :]
        return remote(
            mine if owner is j else source, source, ag_send.at[number], ag_recv.at[number], (i, to)
        )

    gather = [
        move(0, j, 0, edge, right),
        move(1, j, rows - edge, edge, left),
        move(2, j, edge, rows - 2 * edge, head_at(2)),
        move(3, j, edge, rows - edge, right),
        move(4, j, 0, rows - edge, left),
    ]
    forward = [move(5, left, 0, edge, right), move(6, right, rows - edge, edge, left)]
    pl.semaphore_wait(barrier, expected)
    pl.when(there(1))(halo.start)
    for copy in gather:
        copy.start()
    pass_on(0)
    for copy in loads:
        copy.start()

    row_id, col_id = iotas(256, 256)
    apart = row_id ^ col_id
    levels = [(apart < size).astype(f32) for size in (8, 16, 32, 64, 128)] + [
        jnp.ones((256, 256), f32)
    ]
    mm[0] = jnp.where(row_id > col_id, levels[0], 0.0).astype(bf16)
    for n in range(5):
        mm[n + 1] = (levels[n + 1] - levels[n]).astype(bf16)
    for n in range(4):
        eq[n] = levels[n + 1].astype(bf16)
    eq[4] = jnp.where(row_id >= col_id, 1.0, 0.0).astype(bf16)

    for copy in loads[12:]:
        copy.wait()
    first = i * rows
    pos = first + lax.broadcasted_iota(jnp.int32, (8, 256), 1)

    def doc_step(n, carry):
        start, found = carry
        found = jnp.where(pos >= start, start, found)
        return start + doc[n], found

    _, found = lax.fori_loop(
        0, doc.shape[0], doc_step, (jnp.int32(0), jnp.zeros((8, 256), jnp.int32)), unroll=8
    )
    start_row = (found - first).astype(f32)
    start_col = jnp.broadcast_to(start_row[0:1, :], (128, 256)).T
    row_f = lax.broadcasted_iota(jnp.int32, (256, 128), 0).astype(f32)
    col_f = lax.broadcasted_iota(jnp.int32, (256, 128), 1).astype(f32)
    for n in range(3):
        taps[n] = jnp.where(row_f - (3 - n) >= start_col, 1.0, 0.0)
    for n in range(2):
        col_n = col_f + 128.0 * n
        neg[:, 128 * n : 128 * n + 128] = jnp.where(
            (col_n <= row_f) & (col_n >= start_col), 0.0, -1e30
        )
    cmask[...] = jnp.where(start_col < 0.0, 1.0, 0.0)

    lane = lax.broadcasted_iota(jnp.int32, (1, 128), 1)
    rate_row = jnp.zeros((1, 128), f32)
    dt_row = jnp.zeros((1, 128), f32)
    for h in every:
        rate_row = jnp.where(lane == h, rate[h], rate_row)
        dt_row = jnp.where(lane == h, dtb[h], dt_row)

    for n in range(2):
        gather[n].wait_recv()
        forward[n].start()

    @pl.when(there(-1))
    def _():
        halo.wait_recv()
        for copy in halo_on:
            copy.start()

    @pl.when(i == 0)
    def _():
        xg[:, 0:HALO, :] = jnp.zeros((4, HALO, feat), bf16)

    hear(0)
    pass_on(1)

    for copy in loads[:9]:
        copy.wait()
    wab_t = jnp.concatenate(
        [wab[0].astype(f32), wab[1].astype(f32), jnp.zeros((120, wab.shape[2]), f32)], axis=0
    )
    wall[:, 768:896] = wab_t.T.astype(bf16)

    def slice_dot(slot, begin, end):
        weights = wall[pl.ds(pl.multiple_of(slot * feat, feat), feat), begin:end]
        return dot(xg[slot], weights)

    def rounded(value):
        return value.astype(bf16).astype(f32)

    acc[...] = slice_dot(j, 0, 1152)
    hear(1)
    pass_on(2)
    @pl.when(there(-1))
    def _():
        for copy in halo_on:
            copy.wait_recv()

    gather[3].wait_recv()
    acc[...] += slice_dot(left, 0, 1152)
    gather[4].wait_recv()
    acc[...] += slice_dot(right, 0, 1152)
    for copy in (gather[2], forward[0], forward[1]):
        copy.wait_recv()
    acc[:, 768:896] += slice_dot(head_at(2), 768, 896)
    acc[:, 0:256] = rounded(acc[:, 0:256] + slice_dot(head_at(2), 0, 256))
    acc[:, 256:768] = rounded(acc[:, 256:768] + slice_dot(head_at(2), 256, 768))

    def short_conv(col, tap):
        cols = slice(col, col + 128)
        weights = conv[:, tap : tap + 128]
        total = acc[HALO:, cols] * weights[3:4]
        for n in range(3):
            total += acc[HALO - 3 + n : HALO - 3 + n + rows, cols] * weights[n : n + 1] * taps[n]
        return silu(total)

    def unit(matrix):
        return matrix * lax.rsqrt(jnp.sum(matrix * matrix, axis=-1, keepdims=True) + 1e-06)


    k_unit = [unit(short_conv(128 * n, 128 * n)) for n in range(2)]
    k_bf = [k.astype(bf16) for k in k_unit]
    k_dots = [dot_t(k, k) for k in k_bf]
    k_trans = [k.T for k in k_unit]
    ab = acc[HALO:, 768:896]
    pre = ab + dt_row
    gate = -rate_row * (jnp.maximum(pre, 0.0) + jnp.log1p(jnp.exp(-jnp.abs(pre))))
    beta = 1.0 / (1.0 + jnp.exp(-ab))
    g1 = gate.astype(bf16)
    g2 = (gate - g1.astype(f32)).astype(bf16)
    g3 = (gate - g1.astype(f32) - g2.astype(f32)).astype(bf16)
    tri = eq[4]
    cum = dot(tri, g1) + dot(tri, g2) + dot(tri, g3)
    cum_row = cum.T
    carried = jnp.exp(cum) * cmask[...]

    def decay_of(h):
        return jnp.exp(cum[:, h : h + 1] - cum_row[h : h + 1, :] + neg[...])

    last_rows = []
    for h in every:
        kh = h // 2
        decay = decay_of(h)
        b_col = beta[:, 4 + h : 5 + h]
        abuf[h] = (k_dots[kh] * decay * b_col).astype(bf16)
        last_rows.append(decay[rows - 1 : rows, :])
        kvb[h, :, 0:128] = (k_unit[kh] * (b_col * carried[:, h : h + 1])).astype(bf16)
        kvb[h, :, 128:256] = (short_conv(256 + 128 * h, 256 + 128 * h) * b_col).astype(bf16)

    def expand(compact, level):
        size = compact.shape[0]
        return jnp.concatenate([compact.astype(bf16)] * (256 // size), axis=0) * eq[level]

    row16, col16 = iotas(16, 256)
    eye16 = (row16 == (col16 & 15)).astype(f32)
    a8 = [abuf[h] * mm[0] for h in every]
    a8c = [sum(a8[h][16 * n : 16 * n + 16, :] for n in range(1, 16)) + a8[h][0:16, :] for h in every]
    p2 = [dot(a8c[h], a8[h]) for h in every]
    p2f = [expand(p2[h], 0) for h in every]
    x1 = [eye16 - a8c[h].astype(f32) for h in every]
    x2 = [x1[h] + dot(x1[h].astype(bf16), p2f[h]) for h in every]
    p4 = [dot(p2[h].astype(bf16), p2f[h]) for h in every]
    p4f = [expand(p4[h], 0) for h in every]
    d = [x2[h] + dot(x2[h].astype(bf16), p4f[h]) for h in every]
    y = [dot(d[h].astype(bf16), abuf[h] * mm[1]) for h in every]
    d = [d[h] - dot(y[h].astype(bf16), expand(d[h], 0)) for h in every]
    for n, size in enumerate((16, 32, 64)):
        odd = (lax.broadcasted_iota(jnp.int32, (1, 256), 1) & size) != 0
        y = [dot(d[h].astype(bf16), abuf[h] * mm[n + 2]) for h in every]
        z = [dot(y[h].astype(bf16), expand(d[h], n)) for h in every]
        d = [
            jnp.concatenate([jnp.where(odd, 0.0, d[h]), jnp.where(odd, d[h], 0.0) - z[h]], axis=0)
            for h in every
        ]
    upper = [d[h][:, 0:128].astype(bf16) for h in every]
    lower = [d[h][:, 128:256].astype(bf16) for h in every]
    x_up = [dot(upper[h], kvb[h, 0:128, :]).astype(bf16) for h in every]
    y = [dot(lower[h], abuf[h, 128:256, 0:128]).astype(bf16) for h in every]
    x_low = [dot(lower[h], kvb[h, 128:256, :]) for h in every]
    for h in every:
        wub[h, 0:128, :] = x_up[h]
        wub[h, 128:256, :] = (x_low[h] - dot(y[h], x_up[h])).astype(bf16)

    row_k, col_k = iotas(128, 128)
    for h in every:
        k_last = (k_trans[h // 2] * last_rows[h]).astype(bf16)
        step = dot(k_last, wub[h])
        passed = jnp.where(row_k == col_k, carried[rows - 1 : rows, h : h + 1], 0.0)
        to_s[h, :, 0:128] = (passed - step[:, 0:128]).astype(bf16)
        to_s[h, :, 128:256] = step[:, 128:256].astype(bf16)

    hear(2)
    to_copy = [
        remote(to_s.at[2 - 2 * core + n], pair.at[core, n], to_send.at[n], to_recv.at[n], mate)
        for n in range(2)
    ]
    for copy in to_copy:
        copy.start()
    for n in range(2):
        pair[core, n] = to_s[2 * core + n]
    next_copy, after_copy = [], []
    for n in range(2):
        to_copy[n].wait_recv()
        both = dot(pair[1, n, :, 0:128], pair[0, n])
        chip_s[n, :, 0:128] = both[:, 0:128].astype(bf16)
        offset = (both[:, 128:256] + pair[1, n, :, 128:256].astype(f32)).astype(bf16)
        chip_s[n, :, 128:256] = offset
        off_s[n] = offset
        after_copy.append(
            remote(off_s.at[n], off_r.at[n], off_send.at[n], off_recv.at[n], (ctx_at(4), j))
        )
        next_copy.append(
            remote(chip_s.at[n], chip_r.at[n], chip_send.at[n], chip_recv.at[n], (ctx_at(2), j))
        )
        pl.when(there(4))(after_copy[n].start)
        pl.when(there(2))(next_copy[n].start)

    q_cols = slice(896, 1152)
    acc[:, q_cols] = rounded(acc[:, q_cols] + slice_dot(head_at(2), 896, 1152))
    q_unit = [unit(short_conv(896 + 128 * n, 768 + 128 * n)) * (DK**-0.5) for n in range(2)]
    q_dots = [dot_t(q_unit[n].astype(bf16), k_bf[n]) for n in range(2)]
    for h in every:
        seen = dot((q_dots[h // 2] * decay_of(h)).astype(bf16), wub[h])
        reader[h] = (q_unit[h // 2] * carried[:, h : h + 1] - seen[:, 0:128]).astype(bf16)
        local[h] = seen[:, 128:256]

    for copy in loads[9:12]:
        copy.wait()
    z_in = jnp.zeros((rows, 512), f32)
    for n in range(4):
        z_in += dot(xg[n, HALO:, :], wz[feat * n : feat * n + feat, :])
    gain_row = gain[...].reshape(1, 128)
    z_in = silu(rounded(z_in))
    for h in every:
        zbuf[:, 128 * h : 128 * h + 128] = z_in[:, 128 * h : 128 * h + 128] * gain_row

    use_copy = [
        remote(use_s.at[n], s_use.at[2 * core + n], use_send.at[n], use_recv.at[n], mate)
        for n in range(2)
    ]
    first_core = core == 0

    @pl.when(i < 2)
    def _():
        chip_r[...] = jnp.zeros(chip_r.shape, bf16)

    @pl.when(i < 4)
    def _():
        off_r[...] = jnp.zeros(off_r.shape, bf16)

    for n in range(2):
        pl.when(there(-4))(after_copy[n].wait_recv)
        pl.when(there(-2))(next_copy[n].wait_recv)
        s_in = dot(chip_r[n, :, 0:128], off_r[n]) + chip_r[n, :, 128:256].astype(f32)
        s_mid = dot(pair[0, n, :, 0:128], s_in.astype(bf16)) + pair[0, n, :, 128:256].astype(f32)
        use_s[n] = jnp.where(first_core, s_mid, s_in).astype(bf16)
        use_copy[n].start()
        s_use[2 * core + n] = jnp.where(first_core, s_in, s_mid).astype(bf16)
    for copy in use_copy:
        copy.wait_recv()

    chunks = 4
    chunk = rows // chunks
    rs_copy = []
    for c in range(chunks):
        span = slice(chunk * c, chunk * c + chunk)
        gated = []
        for h in every:
            attended = dot(reader[h, span, :], s_use[h]) + local[h, span, :]
            scale = lax.rsqrt(jnp.mean(attended * attended, axis=-1, keepdims=True) + 1e-06)
            gated.append((attended * scale * zbuf[span, 128 * h : 128 * h + 128]).astype(bf16))
        gated = jnp.concatenate(gated, axis=1)
        for n, d_step in enumerate((2, 1, 3)):
            slot = head_at(d_step)
            weights = wo[:, pl.ds(pl.multiple_of(slot * feat, feat), feat)]
            obuf[n, span, :] = dot(gated, weights).astype(bf16)
            copy = remote(
                obuf.at[n, pl.ds(chunk * c, chunk), :],
                rbuf.at[n, pl.ds(chunk * c, chunk), :],
                rs_send.at[c, n],
                rs_recv.at[c, n],
                (i, slot),
            )
            copy.start()
            rs_copy.append(copy)
        osum[span, :] = dot(gated, wo[:, pl.ds(pl.multiple_of(j * feat, feat), feat)])
    for c in range(chunks):
        span = slice(chunk * c, chunk * c + chunk)
        for copy in rs_copy[3 * c : 3 * c + 3]:
            copy.wait_recv()
        total = osum[span, :]
        for n in range(3):
            total += rbuf[n, span, :].astype(f32)
        out[span, :] = total.astype(bf16)

    gathers = gather + forward
    for copy in gathers + to_copy + use_copy + rs_copy:
        copy.wait_send()
    for step, copies in ((1, [halo]), (-1, halo_on), (2, next_copy), (4, after_copy)):

        @pl.when(there(step))
        def _(copies=copies):
            for copy in copies:
                copy.wait_send()


def body(n_ctx, n_head, *arrays):
    (
        tokens,
        q_weight,
        k_weight,
        v_weight,
        z_weight,
        a_weight,
        b_weight,
        conv_q,
        conv_k,
        conv_v,
        decay_rate,
        dt_bias,
        norm_gain,
        out_weight,
        doc_lengths,
    ) = arrays
    rows, feat = tokens.shape
    hbm = pl.BlockSpec(memory_space=pltpu.HBM)
    vmem = pltpu.VMEM
    dma = pltpu.SemaphoreType.DMA
    return pl.pallas_call(
        lambda *refs: layer_kernel(n_ctx, n_head, *refs),
        out_shape=pltpu.VMEM((rows, feat), bf16),
        in_specs=[hbm] * 15,
        out_specs=pl.BlockSpec(memory_space=pltpu.VMEM),
        scratch_shapes=[
            pltpu.SMEM((64,), jnp.int32),
            pltpu.SMEM((4,), f32),
            pltpu.SMEM((4,), f32),
            vmem((4, HALO + rows, feat), bf16),
            vmem((1024, 1152), bf16),
            vmem((1024, 512), bf16),
            vmem((2, 4, 1024), bf16),
            vmem((512, 1024), bf16),
            vmem((4, 1024), f32),
            vmem((128,), f32),
            vmem((HALO + rows, 1152), f32),
            vmem((rows, 512), f32),
            vmem((5, 256, 256), bf16),
            vmem((6, 256, 256), bf16),
            vmem((3, 256, 128), f32),
            vmem((256, 256), f32),
            vmem((256, 128), f32),
            vmem((4, 256, 256), bf16),
            vmem((4, 256, 256), bf16),
            vmem((4, 256, 256), bf16),
            vmem((4, 256, 128), bf16),
            vmem((4, 256, 128), f32),
            vmem((4, 128, 256), bf16),
            vmem((2, 2, 128, 256), bf16),
            vmem((2, 128, 256), bf16),
            vmem((2, 128, 256), bf16),
            vmem((2, 128, 128), bf16),
            vmem((2, 128, 128), bf16),
            vmem((2, 128, 128), bf16),
            vmem((4, 128, 128), bf16),
            vmem((3, rows, feat), bf16),
            vmem((3, rows, feat), bf16),
            vmem((rows, feat), f32),
            dma((15,)),
            dma((4,)),
            dma((4,)),
            dma((7,)),
            dma((7,)),
            dma((2,)),
            dma((2,)),
            dma((2,)),
            dma((2,)),
            dma((2,)),
            dma((2,)),
            dma((2,)),
            dma((2,)),
            dma((4, 3)),
            dma((4, 3)),
            pltpu.SemaphoreType.REGULAR((3,)),
        ],
        compiler_params=pltpu.CompilerParams(
            collective_id=0, has_side_effects=True, vmem_limit_bytes=60 * 1024 * 1024
        ),
        name="delta_layer",
    )(
        doc_lengths,
        decay_rate,
        dt_bias,
        tokens,
        q_weight,
        k_weight,
        v_weight,
        z_weight,
        a_weight.T,
        b_weight.T,
        conv_q,
        conv_k,
        conv_v,
        norm_gain,
        out_weight,
    )


def solution(mesh):
    n_ctx, n_head = mesh.shape["ctx"], mesh.shape["head"]
    return jax.shard_map(
        lambda *arrays: body(n_ctx, n_head, *arrays),
        mesh=mesh,
        in_specs=(
            P("ctx", "head"),
            P(None, "head"),
            P(None, "head"),
            P(None, "head"),
            P(None, "head"),
            P(None, "head"),
            P(None, "head"),
            P(None, "head"),
            P(None, "head"),
            P(None, "head"),
            P("head"),
            P("head"),
            P(),
            P("head", None),
            P(),
        ),
        out_specs=P("ctx", "head"),
        check_vma=False,
    )
```
